32 devices in a mesh: groups: 2 (over x), fsdp: 4 (over z), tensor: 4 (over y, core).
Axes of the slice: x: 2, y: 2, z: 4, core: 2. Of those that a mesh axis runs over, the one named last changes fastest.
Arguments:
- queries: bfloat16 [8, 64, 8192], P(None, ('groups', 'fsdp'), 'tensor'), parts along dimension 1, may hold values from -120 to 120
- cache: bfloat16 [64, 2, 8, 512, 128], P(('groups', 'fsdp', 'tensor')), parts along dimension 0, may hold values from -4 to 4
- decoded_key_value: bfloat16 [8, 64, 2048], P(None, ('groups', 'fsdp'), 'tensor'), parts along dimension 1, may hold values from -8 to 8
- lengths: int32 [64], P(('groups', 'fsdp', 'tensor')), parts along dimension 0, may hold values from 1 to 512, as said below
- frozen_output_weight: bfloat16 [8192, 8192], P('tensor'), may hold values from -0.0625 to 0.0625
- adapter_down_weight: bfloat16 [8192, 64], P('tensor', 'fsdp'), may hold values from -0.0625 to 0.0625
- adapter_up_weight: bfloat16 [64, 8192], P(None, ('fsdp', 'tensor')), may hold values from -0.75 to 0.75
Outputs:
- projected: bfloat16 [8, 64, 8192], P(None, ('groups', 'fsdp', 'tensor')), parts along dimension 1
The draws below stay inside these ranges and needn't reach their ends.
There are 2 independent parts, one for each index of `groups`. The reference program is written for one: setup_inputs(seed, part) draws one part's arguments, and reference() takes and returns one part's arrays. A program takes and returns all parts, laid end to end along the dimension named above; an argument that names none is the same for every part. Nothing has to cross between parts.
Inputs may be any that keep to these rules, and one draw needn't show every extreme that they name: `lengths`: some row has 512 filled slots and some row has 1.
All inputs are finite; a program needn't handle non-finite values.
Results may differ from the reference program's by a relative error of at most 0.0058.
Values may be sent and summed in bfloat16 or wider, within the bound.
No kernel may reach another device: no remote copies, remote signals or barrier semaphores. Data moves between devices by JAX's collectives and lax.ppermute only.
A program may use at most 128 MiB of HBM per device.

```python
import jax
import jax.numpy as jnp
from jax import lax

MODEL_WIDTH = 8192
HEADS = 64
KV_HEADS = 8
HEAD_DIM = 128
ADAPTER_RANK = 64
STEPS = 8
CACHE = 512
ROWS = 32


def first_keys(key):
    shape = (ROWS, 2, KV_HEADS, 1, HEAD_DIM)
    return jnp.clip(jax.random.normal(jax.random.fold_in(key, 101), shape, jnp.float32), -4.0, 4.0)


def draw_cache(key, part):
    leading = first_keys(key)
    key = jax.random.fold_in(key, 3)
    remaining = jax.random.normal(key, (ROWS, 2, KV_HEADS, CACHE - 1, HEAD_DIM), jnp.float32)
    remaining = jnp.clip(remaining, -4.0, 4.0)
    return jnp.concatenate([leading, remaining], axis=3).astype(jnp.bfloat16)


def draw_queries(key, part):
    key = jax.random.fold_in(key, 5)
    values = jnp.clip(jax.random.normal(key, (STEPS, ROWS, MODEL_WIDTH), jnp.float32), -4.0, 4.0)
    return values.astype(jnp.bfloat16)


def draw_decoded_key_value(key, part):
    key = jax.random.fold_in(key, 7)
    values = jnp.clip(2.0 * jax.random.normal(key, (STEPS, ROWS, 2 * KV_HEADS * HEAD_DIM), jnp.float32), -8.0, 8.0)
    return values.astype(jnp.bfloat16)


def draw_lengths(key, part):
    key = jax.random.fold_in(key, 13)
    filled = jax.random.randint(key, (ROWS,), 1, CACHE + 1)
    longest = jax.random.randint(jax.random.fold_in(key, 1), (), 0, ROWS)
    offset = jax.random.randint(jax.random.fold_in(key, 2), (), 0, ROWS - 1)
    shortest = (longest + 1 + offset) % ROWS
    return filled.at[longest].set(CACHE).at[shortest].set(1).astype(jnp.int32)


def levels(rng, extent, split, least, largest):
    loudness = 1.0
    for position, blocks in split:
        steps = jax.random.uniform(jax.random.fold_in(jax.random.fold_in(rng, 6), position), (blocks,), jnp.float32, least / len(split), largest / len(split))
        loudness = loudness * jnp.repeat(jnp.exp(steps), extent[position] // blocks).reshape((-1,) + (1,) * (len(extent) - 1 - position))
    return loudness


def noise(key, shape, scale, reach, cuts=(), kind=jnp.bfloat16):
    entries = scale * jax.random.normal(key, shape, jnp.float32)
    if cuts:
        entries = entries * levels(key, shape, cuts, -0.22, 0.18)
    return jnp.clip(entries, -reach, reach).astype(kind)


def setup_inputs(seed: int = 0, part: int = 0) -> dict:
    seeds = jax.random.split(jax.random.key(seed), 8)
    part_keys = jax.random.split(jax.random.fold_in(seeds[7], part), 8)
    return {
        "queries": draw_queries(jax.random.fold_in(jax.random.fold_in(seeds[7], part), 71), part),
        "cache": draw_cache(jax.random.fold_in(jax.random.fold_in(seeds[7], part), 71), part),
        "decoded_key_value": draw_decoded_key_value(jax.random.fold_in(jax.random.fold_in(seeds[7], part), 71), part),
        "lengths": draw_lengths(jax.random.fold_in(jax.random.fold_in(seeds[7], part), 71), part),
        "frozen_output_weight": noise(seeds[4], (MODEL_WIDTH, MODEL_WIDTH), MODEL_WIDTH ** -0.5, 0.0625, ((0, 4),)),
        "adapter_down_weight": noise(seeds[5], (MODEL_WIDTH, ADAPTER_RANK), MODEL_WIDTH ** -0.5, 0.0625, ((0, 4), (1, 4))),
        "adapter_up_weight": noise(seeds[6], (ADAPTER_RANK, MODEL_WIDTH), ADAPTER_RANK ** -0.5, 0.75, ((1, 16),)),
    }


adapter_scale = 2.0


def attend_row(pieces):
    query_row, cache_row, new_row, length = pieces
    group = HEADS // KV_HEADS
    kv_width = KV_HEADS * HEAD_DIM
    scale = HEAD_DIM ** -0.5
    grouped = query_row.astype(jnp.float32).reshape(STEPS, KV_HEADS, group, HEAD_DIM)
    cache_keys = cache_row[0].astype(jnp.float32)
    cache_values = cache_row[1].astype(jnp.float32)
    new_keys = new_row[:, :kv_width].astype(jnp.float32).reshape(STEPS, KV_HEADS, HEAD_DIM)
    new_values = new_row[:, kv_width:].astype(jnp.float32).reshape(STEPS, KV_HEADS, HEAD_DIM)
    cache_scores = jnp.einsum("skgd,kcd->skgc", grouped, cache_keys, precision=lax.Precision.HIGHEST) * scale
    new_scores = jnp.einsum("skgd,nkd->skgn", grouped, new_keys, precision=lax.Precision.HIGHEST) * scale
    valid = (jnp.arange(CACHE, dtype=jnp.int32) < length)[None, None, None, :]
    step_ids = jnp.arange(STEPS, dtype=jnp.int32)
    causal = (step_ids[None, :] <= step_ids[:, None])[:, None, None, :]
    masked_cache = jnp.where(valid, cache_scores, -1e30)
    masked_new = jnp.where(causal, new_scores, -1e30)
    highest = jnp.maximum(masked_cache.max(-1), masked_new.max(-1))[..., None]
    cache_probs = jnp.where(valid, jnp.exp(masked_cache - highest), 0.0)
    new_probs = jnp.where(causal, jnp.exp(masked_new - highest), 0.0)
    totals = cache_probs.sum(-1) + new_probs.sum(-1)
    mixed = jnp.einsum("skgc,kcd->skgd", cache_probs, cache_values, precision=lax.Precision.HIGHEST)
    mixed = mixed + jnp.einsum("skgn,nkd->skgd", new_probs, new_values, precision=lax.Precision.HIGHEST)
    return (mixed / totals[..., None]).reshape(STEPS, MODEL_WIDTH).astype(jnp.bfloat16)


def reference(queries, cache, decoded_key_value, lengths, frozen_output_weight, adapter_down_weight, adapter_up_weight):
    weight_delta = jnp.dot(adapter_down_weight, adapter_up_weight, preferred_element_type=jnp.float32)
    combined_output_weight = (frozen_output_weight.astype(jnp.float32) + adapter_scale * weight_delta).astype(jnp.bfloat16)
    attended = lax.map(attend_row, (jnp.transpose(queries, (1, 0, 2)), cache, jnp.transpose(decoded_key_value, (1, 0, 2)), lengths.astype(jnp.int32)))
    attended = jnp.transpose(attended, (1, 0, 2)).reshape(STEPS * ROWS, MODEL_WIDTH)
    projected = jnp.dot(attended, combined_output_weight, preferred_element_type=jnp.float32)
    return projected.astype(jnp.bfloat16).reshape(STEPS, ROWS, MODEL_WIDTH)
```

```python
import functools

import jax
import jax.numpy as jnp
from jax import lax
from jax.experimental import pallas as pl
from jax.experimental.pallas import tpu as pltpu
from jax.sharding import PartitionSpec as P

HEADS = 64
KV_HEADS = 8
HEAD_DIM = 128
GROUP = HEADS // KV_HEADS
RANK = 64
SCALE = 2.0
CHUNKS = 2
BF16 = jnp.bfloat16
F32 = jnp.float32
VMEM = pl.BlockSpec(memory_space=pltpu.VMEM)
SMEM = pl.BlockSpec(memory_space=pltpu.SMEM)
ROW_ROW = (((1,), (1,)), ((), ()))


def dot(a, b):
    return jnp.dot(a, b, preferred_element_type=F32)


def dot_rows(a, b):
    return lax.dot_general(a, b, ROW_ROW, preferred_element_type=F32)


def params(mib=24):
    return pltpu.CompilerParams(vmem_limit_bytes=mib * 2**20)


def split(x):
    high = x.astype(BF16)
    return high, (x - high.astype(F32)).astype(BF16)


def log2(n):
    return n.bit_length() - 1


def pack_kernel(query_ref, new_ref, down_ref, up_ref, *out_refs, parts, own, steps):
    *block_refs, factor_ref = out_refs
    me = lax.axis_index("tensor")
    rows = parts * own
    count = steps * rows
    i = lax.broadcasted_iota(jnp.int32, (count, count), 0)
    j = lax.broadcasted_iota(jnp.int32, (count, count), 1)
    step_out = i & (steps - 1)
    row_out = (i >> log2(steps)) & (own - 1)
    part_out = (i >> log2(steps * own)) ^ me
    source = step_out * rows + part_out * own + row_out
    select = jnp.where(source == j, 1.0, 0.0).astype(BF16)
    queries = query_ref[...].reshape(count, query_ref.shape[2])
    new = new_ref[...].reshape(count, new_ref.shape[2])
    queries = dot(select, queries)
    new = dot(select, new)
    heads = queries.shape[1] // HEAD_DIM
    pieces = new.shape[1] // HEAD_DIM
    tall = own * steps
    for k, block_ref in enumerate(block_refs):
        q = queries[k * tall : (k + 1) * tall]
        n = new[k * tall : (k + 1) * tall]
        tiles = [
            q[r * steps : (r + 1) * steps, h * HEAD_DIM : (h + 1) * HEAD_DIM]
            for r in range(own)
            for h in range(heads)
        ]
        tiles += [n[:, c * HEAD_DIM : (c + 1) * HEAD_DIM] for c in range(pieces)]
        block_ref[...] = jnp.concatenate(tiles, axis=0).astype(BF16)
    slot, depth = down_ref.shape[1], down_ref.shape[0]
    a = lax.broadcasted_iota(jnp.int32, (slot, slot), 0)
    b = lax.broadcasted_iota(jnp.int32, (slot, slot), 1)
    eye = jnp.where(a == b, 1.0, 0.0).astype(BF16)
    factor_ref[0:slot, :] = dot_rows(eye, down_ref[...]).astype(BF16)
    cut = up_ref.shape[1]
    per = depth // cut
    for c in range(per):
        lanes = slice(c * cut, (c + 1) * cut)
        tall = RANK // per
        factor_ref[slot + c * tall : slot + (c + 1) * tall, lanes] = up_ref[c * tall : (c + 1) * tall, :]


def attend_kernel(length_ref, *refs, parts, own, steps):
    block_refs = refs[:parts]
    cache_ref = refs[parts]
    out_refs = refs[parts + 1 : 2 * parts + 1]
    held_ref, attended_ref = refs[2 * parts + 1 :]
    me = lax.axis_index("tensor")
    for k in range(parts):
        held_ref[me ^ k] = block_refs[k][...]
    heads = HEADS // parts
    pieces = 2 * KV_HEADS // parts
    query_rows = own * heads * steps
    tall = own * steps
    slots = cache_ref.shape[3]
    together = min(heads, GROUP)
    scale = HEAD_DIM ** (-0.5)

    def piece(c):
        start = query_rows + (c % pieces) * tall
        return held_ref[c // pieces, start : start + tall, :]

    queries_count = GROUP * steps
    slot_ids = lax.broadcasted_iota(jnp.int32, (queries_count, slots), 1)
    step_ids = lax.broadcasted_iota(jnp.int32, (queries_count, tall), 0) & (steps - 1)
    new_ids = lax.broadcasted_iota(jnp.int32, (queries_count, tall), 1)
    for r in range(own):
        valid = slot_ids < length_ref[r]
        past = new_ids - r * steps
        causal = (past >= 0) & (past <= step_ids)
        for g in range(KV_HEADS):
            parts_q = []
            for first in range(g * GROUP, (g + 1) * GROUP, together):
                start = (r * heads + first % heads) * steps
                parts_q.append(held_ref[first // heads, start : start + together * steps, :])
            q = parts_q[0] if len(parts_q) == 1 else jnp.concatenate(parts_q, axis=0)
            old_scores = jnp.where(valid, dot_rows(q, cache_ref[r, 0, g]) * scale, -1e30)
            new_scores = jnp.where(causal, dot_rows(q, piece(g)) * scale, -1e30)
            highest = jnp.maximum(
                old_scores.max(-1, keepdims=True), new_scores.max(-1, keepdims=True)
            )
            old = jnp.exp(old_scores - highest)
            new = jnp.exp(new_scores - highest)
            total = old.sum(-1, keepdims=True) + new.sum(-1, keepdims=True)
            old = jnp.concatenate(split(old), axis=0)
            new = jnp.concatenate(split(new), axis=0)
            mixed = dot(old, cache_ref[r, 1, g]) + dot(new, piece(KV_HEADS + g))
            mixed = (mixed[:queries_count] + mixed[queries_count:]) / total
            for h in range(GROUP):
                head = g * GROUP + h
                lane = (head % heads) * HEAD_DIM
                attended_ref[
                    head // heads, r * steps : (r + 1) * steps, lane : lane + HEAD_DIM
                ] = mixed[h * steps : (h + 1) * steps]
    for k in range(parts):
        out_refs[k][...] = attended_ref[me ^ k].astype(BF16)


def collect_kernel(*refs, slot):
    factor_refs = refs[:-2]
    down_ref, up_ref = refs[-2:]
    me = lax.axis_index("fsdp")
    cut = up_ref.shape[2]
    per = down_ref.shape[1] // cut
    tall = RANK // per
    for k, factor_ref in enumerate(factor_refs):
        down_ref[pl.ds(pl.multiple_of((me ^ k) * slot, slot), slot), :] = factor_ref[0:slot, :]
        for c in range(per):
            up_ref[k, c * tall : (c + 1) * tall, :] = factor_ref[
                slot + c * tall : slot + (c + 1) * tall, c * cut : (c + 1) * cut
            ]


def project_kernel(*refs, parts, with_low):
    attended_refs = refs[:parts]
    weight_ref = refs[parts]
    rest = refs[parts + 1 :]
    if with_low:
        down_ref, rest = rest[0], rest[1:]
    keep_ref, send_ref = rest[0], rest[1]
    rows = jnp.concatenate([a[...] for a in attended_refs], axis=0)
    half = rows.shape[0] // 2
    out = dot(rows, weight_ref[...])
    keep_ref[...] = out[:half]
    send_ref[...] = out[half:].astype(BF16)
    if with_low:
        low_keep_ref, low_send_ref = rest[2], rest[3]

        @pl.when(pl.program_id(0) == 0)
        def _():
            low = dot_rows(rows, down_ref[...])
            low_keep_ref[...] = low[:half]
            high, rest_low = split(low[half:])
            low_send_ref[...] = jnp.concatenate([high, rest_low], axis=1)


def project(attended, weight, chunk, tile, down=None):
    parts = len(attended)
    tall, depth = attended[0].shape
    width = weight.shape[1] // CHUNKS
    half = parts * tall // 2
    tiles = width // tile
    out_shape = [
        jax.ShapeDtypeStruct((half, width), F32),
        jax.ShapeDtypeStruct((half, width), BF16),
    ]
    out_specs = [
        pl.BlockSpec((half, tile), lambda j: (0, j)),
        pl.BlockSpec((half, tile), lambda j: (0, j)),
    ]
    whole = lambda shape: pl.BlockSpec(shape, lambda j: (0, 0))
    in_specs = [whole((tall, depth))] * parts
    in_specs += [pl.BlockSpec((depth, tile), lambda j: (0, chunk * tiles + j))]
    args = [*attended, weight]
    if down is not None:
        in_specs += [whole(down.shape)]
        args += [down]
        out_shape += [
            jax.ShapeDtypeStruct((half, RANK), F32),
            jax.ShapeDtypeStruct((half, 2 * RANK), BF16),
        ]
        out_specs += [whole((half, RANK)), whole((half, 2 * RANK))]
    return pl.pallas_call(
        functools.partial(project_kernel, parts=parts, with_low=down is not None),
        grid=(tiles,),
        in_specs=in_specs,
        out_specs=out_specs,
        out_shape=out_shape,
        compiler_params=params(),
        name="project",
    )(*args)


def fold_low(keep, got):
    return keep + got[:, :RANK].astype(F32) + got[:, RANK:].astype(F32)


def finish_kernel(*refs, sets, cut, own, steps):
    sum_refs, refs = refs[: 2 * CHUNKS], refs[2 * CHUNKS :]
    low_keep_ref, low_got_ref, refs = refs[0], refs[1], refs[2:]
    *up_refs, out_ref, extra_ref = refs
    me, place = lax.axis_index("tensor"), lax.axis_index("fsdp")
    low = SCALE * fold_low(low_keep_ref[...], low_got_ref[...])
    tall = low.shape[0]
    low = jnp.concatenate(split(low), axis=0)
    if len(up_refs) == 1:
        both = dot(low, up_refs[0][...])
        extra_ref[...] = both[:tall] + both[tall:]
    else:
        for kt, up_ref in enumerate(up_refs):
            for kf in range(up_ref.shape[0]):
                both = dot(low, up_ref[kf])
                start = pl.multiple_of(((place ^ kf) * sets + (me ^ kt)) * cut, cut)
                extra_ref[:, pl.ds(start, cut)] = both[:tall] + both[tall:]
    width = sum_refs[0].shape[1]
    for c in range(CHUNKS):
        lanes = slice(c * width, (c + 1) * width)
        total = sum_refs[2 * c][...] + sum_refs[2 * c + 1][...].astype(F32) + extra_ref[:, lanes]
        total = total.astype(BF16)
        for r in range(own):
            out_ref[:, r, lanes] = total[r * steps : (r + 1) * steps]


def shards(queries, cache, new, lengths, weight, down, up):
    parts, spread = lax.axis_size("tensor"), lax.axis_size("fsdp")
    steps, rows, width = queries.shape
    own = rows // parts
    tall = own * steps
    depth, slot = down.shape
    cut = up.shape[1]
    heads, pieces = width // HEAD_DIM, new.shape[2] // HEAD_DIM
    swap = lambda x, axis, k: lax.ppermute(
        x, axis, [(i, i ^ k) for i in range(lax.axis_size(axis))]
    )

    block = jax.ShapeDtypeStruct((own * heads * steps + pieces * tall, HEAD_DIM), BF16)
    *blocks, factors = pl.pallas_call(
        functools.partial(pack_kernel, parts=parts, own=own, steps=steps),
        in_specs=[VMEM] * 4,
        out_specs=[VMEM] * (parts + 1),
        out_shape=[block] * parts + [jax.ShapeDtypeStruct((slot + RANK, depth), BF16)],
        compiler_params=params(),
        name="pack",
    )(queries, new, down, up)
    blocks = [blocks[0]] + [swap(blocks[k], "tensor", k) for k in range(1, parts)]
    factors = [factors] + [swap(factors, "fsdp", k) for k in range(1, spread)]

    attended = pl.pallas_call(
        functools.partial(attend_kernel, parts=parts, own=own, steps=steps),
        in_specs=[SMEM] + [VMEM] * (parts + 1),
        out_specs=[VMEM] * parts,
        out_shape=[jax.ShapeDtypeStruct((tall, width), BF16)] * parts,
        scratch_shapes=[
            pltpu.VMEM((parts,) + block.shape, BF16),
            pltpu.VMEM((parts, tall, width), F32),
        ],
        compiler_params=params(),
        name="attend",
    )(lengths, *blocks, cache)
    attended = [attended[0]] + [swap(attended[k], "tensor", k) for k in range(1, parts)]

    down_rows, ups = pl.pallas_call(
        functools.partial(collect_kernel, slot=slot),
        in_specs=[VMEM] * spread,
        out_specs=[VMEM] * 2,
        out_shape=[
            jax.ShapeDtypeStruct((RANK, depth), BF16),
            jax.ShapeDtypeStruct((spread, RANK, cut), BF16),
        ],
        compiler_params=params(),
        name="collect",
    )(*factors)
    if cut % HEAD_DIM:
        up_sets = {0: lax.all_gather(up, ("fsdp", "tensor"), axis=1, tiled=True)}
    else:
        up_sets = {0: ups}
        bit = parts // 2
        while bit:
            up_sets |= {k ^ bit: swap(u, "tensor", bit) for k, u in list(up_sets.items())}
            bit //= 2

    order = sorted(range(parts), key=lambda k: format(k, "08b")[::-1])
    attended = [attended[k] for k in order]
    sums = []
    low = None
    for c in range(CHUNKS):
        keep, send, *lows = project(
            attended, weight, c, min(512, weight.shape[1] // CHUNKS), down_rows if c == 0 else None
        )
        bit = 1
        while True:
            got = swap(send, "tensor", bit)
            if lows:
                low_keep, low_send = lows
                low_got = swap(low_send, "tensor", bit)
            bit *= 2
            if bit == parts:
                break
            both = keep + got.astype(F32)
            half = both.shape[0] // 2
            keep, send = both[:half], both[half:].astype(BF16)
            if lows:
                low_both = fold_low(low_keep, low_got)
                lows = low_both[:half], jnp.concatenate(split(low_both[half:]), axis=1)
        sums += [keep, got]
        if lows:
            low = [low_keep, low_got]

    return pl.pallas_call(
        functools.partial(finish_kernel, sets=parts, cut=cut, own=own, steps=steps),
        in_specs=[VMEM] * (2 * CHUNKS + 2 + len(up_sets)),
        out_specs=VMEM,
        out_shape=jax.ShapeDtypeStruct((steps, own, weight.shape[1]), BF16),
        scratch_shapes=[pltpu.VMEM((tall, weight.shape[1]), F32)],
        compiler_params=params(),
        name="finish",
    )(*sums, *low, *[up_sets[k] for k in range(len(up_sets))])


def solution(mesh):
    return jax.shard_map(
        shards,
        mesh=mesh,
        in_specs=(
            P(None, ("groups", "fsdp"), "tensor"),
            P(("groups", "fsdp", "tensor"), None, None, None, None),
            P(None, ("groups", "fsdp"), "tensor"),
            P(("groups", "fsdp", "tensor")),
            P("tensor", None),
            P("tensor", "fsdp"),
            P(None, ("fsdp", "tensor")),
        ),
        out_specs=P(None, ("groups", "fsdp", "tensor"), None),
        check_vma=False,
    )
```

```python
import functools

import jax
import jax.numpy as jnp
from jax import lax
from jax.experimental import pallas as pl
from jax.experimental.pallas import tpu as pltpu
from jax.sharding import PartitionSpec as P

HEADS = 64
KV_HEADS = 8
HEAD_DIM = 128
GROUP = HEADS // KV_HEADS
RANK = 64
SCALE = 2.0
BF16 = jnp.bfloat16
F32 = jnp.float32
VMEM = pl.BlockSpec(memory_space=pltpu.VMEM)
ANY = pl.BlockSpec(memory_space=pl.ANY)
ROW_ROW = (((1,), (1,)), ((), ()))
shape_of = jax.ShapeDtypeStruct


def dot(a, b):
    return jnp.dot(a, b, preferred_element_type=F32)


def dot_rows(a, b):
    return lax.dot_general(a, b, ROW_ROW, preferred_element_type=F32)


def call(kernel, name, ins, outs, scratch=(), mib=16, cost=None):
    specs, args = zip(*ins)
    return pl.pallas_call(
        kernel,
        in_specs=list(specs),
        out_specs=[VMEM] * len(outs),
        out_shape=list(outs),
        scratch_shapes=list(scratch),
        compiler_params=pltpu.CompilerParams(vmem_limit_bytes=mib * 2**20),
        cost_estimate=cost,
        name=name,
    )(*args)


def split(x):
    high = x.astype(BF16)
    return high, (x - high.astype(F32)).astype(BF16)


def log2(n):
    return n.bit_length() - 1


def strip_copy(weight_ref, strip, own_half, index, into_ref, sem):
    width = into_ref.shape[1]
    top = lax.axis_index("tensor") >> (log2(lax.axis_size("tensor")) - 1)
    half = top if own_half else 1 - top
    start = pl.multiple_of((2 * strip + half) * width, width)
    return pltpu.make_async_copy(weight_ref.at[:, pl.ds(start, width)], into_ref, sem.at[index])


def pack_kernel(query_hbm, new_hbm, down_hbm, up_hbm, *refs, parts, own, steps):
    block_refs, factor_ref = refs[:parts], refs[parts]
    query_ref, new_ref, down_ref, up_ref, sem = refs[parts + 1 :]
    copies = [
        pltpu.make_async_copy(a, b, sem.at[i])
        for i, (a, b) in enumerate(
            [(query_hbm, query_ref), (new_hbm, new_ref), (down_hbm, down_ref), (up_hbm, up_ref)]
        )
    ]
    for copy in copies:
        copy.start()
    me = lax.axis_index("tensor")
    count = steps * parts * own
    i = lax.broadcasted_iota(jnp.int32, (count, count), 0)
    j = lax.broadcasted_iota(jnp.int32, (count, count), 1)
    step_out = i & (steps - 1)
    row_out = (i >> log2(steps)) & (own - 1)
    part_out = (i >> log2(steps * own)) ^ me
    source = step_out * (parts * own) + part_out * own + row_out
    select = jnp.where(source == j, 1.0, 0.0).astype(BF16)
    for copy in copies:
        copy.wait()
    queries = dot(select, query_ref[...].reshape(count, query_ref.shape[2]))
    new = dot(select, new_ref[...].reshape(count, new_ref.shape[2]))
    heads = queries.shape[1] // HEAD_DIM
    pieces = new.shape[1] // HEAD_DIM
    tall = own * steps
    for k, block_ref in enumerate(block_refs):
        q = queries[k * tall : (k + 1) * tall]
        n = new[k * tall : (k + 1) * tall]
        tiles = [
            q[r * steps : (r + 1) * steps, h * HEAD_DIM : (h + 1) * HEAD_DIM]
            for r in range(own)
            for h in range(heads)
        ]
        tiles += [n[:, c * HEAD_DIM : (c + 1) * HEAD_DIM] for c in range(pieces)]
        block_ref[...] = jnp.concatenate(tiles, axis=0).astype(BF16)
    slot, depth = down_ref.shape
    cut = up_ref.shape[1]
    per = depth // cut
    tall = RANK // per
    factor_ref[0:slot, :] = down_ref[...]
    for c in range(per):
        factor_ref[slot : slot + tall, c * cut : (c + 1) * cut] = up_ref[c * tall : (c + 1) * tall, :]


def attend_kernel(length_hbm, *refs, parts, own, steps, strips):
    block_refs, refs = refs[:parts], refs[parts:]
    cache_hbm, weight_hbm, refs = refs[0], refs[1], refs[2:]
    out_refs, refs = refs[:parts], refs[parts:]
    strip_refs, refs = refs[:strips], refs[strips:]
    cache_ref, length_ref, held_ref, attended_ref, cache_sem, sem = refs
    length_copy = pltpu.make_async_copy(length_hbm, length_ref, sem.at[strips])
    length_copy.start()
    pairs = KV_HEADS // 2

    def cache_copy(r, p, part):
        two = pl.ds(2 * p, 2)
        return pltpu.make_async_copy(
            cache_hbm.at[r, part, two], cache_ref.at[r, part, two], cache_sem.at[r, p, part]
        )

    for r in range(own):
        for p in range(pairs):
            cache_copy(r, p, 0).start()
            cache_copy(r, p, 1).start()
    weight_copies = [
        strip_copy(weight_hbm, i, False, i, strip_refs[i], sem) for i in range(strips)
    ]
    for copy in weight_copies:
        copy.start()

    me = lax.axis_index("tensor")
    for k in range(parts):
        held_ref[me ^ k] = block_refs[k][...]
    heads = HEADS // parts
    pieces = 2 * KV_HEADS // parts
    query_rows = own * heads * steps
    tall = own * steps
    slots = cache_ref.shape[3]
    together = min(heads, GROUP)
    scale = HEAD_DIM ** (-0.5)
    count = GROUP * steps

    def piece(c):
        start = query_rows + (c % pieces) * tall
        return held_ref[c // pieces, start : start + tall, :]

    def beside(a, b):
        return jnp.concatenate([a, b], axis=1)

    slot_ids = lax.broadcasted_iota(jnp.int32, (2 * count, slots), 1)
    step_ids = lax.broadcasted_iota(jnp.int32, (2 * count, tall), 0) & (steps - 1)
    new_ids = lax.broadcasted_iota(jnp.int32, (2 * count, tall), 1)
    blank = jnp.zeros((count, HEAD_DIM), BF16)
    length_copy.wait()
    for r in range(own):
        valid = slot_ids < length_ref[r]
        past = new_ids - r * steps
        causal = (past >= 0) & (past <= step_ids)
        for p in range(pairs):
            q = []
            for g in (2 * p, 2 * p + 1):
                found = []
                for first in range(g * GROUP, (g + 1) * GROUP, together):
                    start = (r * heads + first % heads) * steps
                    found.append(held_ref[first // heads, start : start + together * steps, :])
                q.append(found[0] if len(found) == 1 else jnp.concatenate(found, axis=0))
            q = jnp.concatenate([beside(q[0], blank), beside(blank, q[1])], axis=0)
            cache_copy(r, p, 0).wait()
            keys = beside(cache_ref[r, 0, 2 * p], cache_ref[r, 0, 2 * p + 1])
            new_keys = beside(piece(2 * p), piece(2 * p + 1))
            old_scores = jnp.where(valid, dot_rows(q, keys) * scale, -1e30)
            new_scores = jnp.where(causal, dot_rows(q, new_keys) * scale, -1e30)
            highest = jnp.maximum(
                old_scores.max(-1, keepdims=True), new_scores.max(-1, keepdims=True)
            )
            old = jnp.exp(old_scores - highest)
            new = jnp.exp(new_scores - highest)
            total = old.sum(-1, keepdims=True) + new.sum(-1, keepdims=True)
            old = jnp.concatenate(split(old), axis=0)
            new = jnp.concatenate(split(new), axis=0)
            cache_copy(r, p, 1).wait()
            values = beside(cache_ref[r, 1, 2 * p], cache_ref[r, 1, 2 * p + 1])
            new_values = beside(piece(KV_HEADS + 2 * p), piece(KV_HEADS + 2 * p + 1))
            mixed = dot(old, values) + dot(new, new_values)
            mixed = (mixed[: 2 * count] + mixed[2 * count :]) / total
            for side in range(2):
                for h in range(GROUP):
                    head = (2 * p + side) * GROUP + h
                    lane = (head % heads) * HEAD_DIM
                    row = side * count + h * steps
                    attended_ref[
                        head // heads, r * steps : (r + 1) * steps, lane : lane + HEAD_DIM
                    ] = mixed[row : row + steps, side * HEAD_DIM : (side + 1) * HEAD_DIM]
    for k in range(parts):
        out_refs[k][...] = attended_ref[me ^ k].astype(BF16)
    for copy in weight_copies:
        copy.wait()


def collect_kernel(*refs, slot):
    *factor_refs, down_ref, up_ref = refs
    me = lax.axis_index("fsdp")
    cut = up_ref.shape[2]
    per = down_ref.shape[1] // cut
    tall = RANK // per
    for k, factor_ref in enumerate(factor_refs):
        down_ref[pl.ds(pl.multiple_of((me ^ k) * slot, slot), slot), :] = factor_ref[0:slot, :]
        for c in range(per):
            up_ref[k, c * tall : (c + 1) * tall, :] = factor_ref[
                slot : slot + tall, c * cut : (c + 1) * cut
            ]


def fetch_kernel(after_ref, weight_hbm, *refs, first):
    *strip_refs, sem = refs
    copies = [
        strip_copy(weight_hbm, first + i, False, i, strip_ref, sem)
        for i, strip_ref in enumerate(strip_refs)
    ]
    for copy in copies:
        copy.start()
    for copy in copies:
        copy.wait()


def project_kernel(*refs, parts, held, ahead, late, first, with_low):
    attended_refs, refs = refs[:parts], refs[parts:]
    held_refs, refs = refs[:held], refs[held:]
    weight_hbm, refs = refs[0], refs[1:]
    if with_low:
        down_ref, refs = refs[0], refs[1:]
    keep_ref, send_ref, refs = refs[0], refs[1], refs[2:]
    if with_low:
        low_keep_ref, low_send_ref, refs = refs[0], refs[1], refs[2:]
    ahead_refs, refs = refs[:ahead], refs[ahead:]
    late_refs, sem = refs[:late], refs[-1]
    copies = [
        strip_copy(weight_hbm, first + i, True, i, ref, sem)
        for i, ref in enumerate([*late_refs, *ahead_refs])
    ]
    for copy in copies:
        copy.start()
    rows = jnp.concatenate([a[...] for a in attended_refs], axis=0)
    half = rows.shape[0] // 2
    if with_low:
        low = dot_rows(rows, down_ref[...])
        low_keep_ref[...] = low[:half]
        low_send_ref[...] = jnp.concatenate(split(low[half:]), axis=1)
    for i, strip_ref in enumerate([*held_refs, *late_refs]):
        if i >= held:
            copies[i - held].wait()
        width = strip_ref.shape[1]
        lanes = slice(i * width, (i + 1) * width)
        out = dot(rows, strip_ref[...])
        keep_ref[:, lanes] = out[:half]
        send_ref[:, lanes] = out[half:].astype(BF16)
    for copy in copies[late:]:
        copy.wait()


def project(attended, held, weight, wide, ahead=0, late=0, first=0, down=None):
    parts = len(attended)
    tall, depth = attended[0].shape
    half = parts * tall // 2
    width = wide * (len(held) + late)
    outs = [shape_of((half, width), F32), shape_of((half, width), BF16)]
    ins = [(VMEM, a) for a in attended] + [(VMEM, h) for h in held] + [(ANY, weight)]
    if down is not None:
        ins += [(VMEM, down)]
        outs += [shape_of((half, RANK), F32), shape_of((half, 2 * RANK), BF16)]
    strip = pltpu.VMEM((depth, wide), BF16)
    outs += [strip] * ahead
    scratch = [strip] * late + [pltpu.SemaphoreType.DMA((max(ahead + late, 1),))]
    kernel = functools.partial(
        project_kernel,
        parts=parts,
        held=len(held),
        ahead=ahead,
        late=late,
        first=first,
        with_low=down is not None,
    )
    cost = pl.CostEstimate(
        flops=2 * parts * tall * depth * width, bytes_accessed=2 * depth * width, transcendentals=0
    )
    return call(kernel, "project", ins, outs, scratch, cost=cost)


def fold_low(keep, got):
    return keep + got[:, :RANK].astype(F32) + got[:, RANK:].astype(F32)


def adapt_kernel(*refs, pieces, sets, ordered):
    low_ref, low_got_ref, refs = refs[0], refs[1], refs[2:]
    keep_refs, refs = refs[:pieces], refs[pieces:]
    got_refs, refs = refs[:pieces], refs[pieces:]
    up_refs, (own_ref, send_ref, extra_ref) = refs[:sets], refs[sets:]
    me, place = lax.axis_index("tensor"), lax.axis_index("fsdp")
    half = low_ref.shape[0] // 2
    got = low_got_ref[...]
    got = jnp.concatenate([got[:, : 2 * RANK], got[:, 2 * RANK :]], axis=0)
    low = SCALE * fold_low(low_ref[...], got)
    low = jnp.concatenate(split(low), axis=0)
    if ordered:
        both = dot(low, up_refs[0][...])
        extra_ref[...] = both[: 2 * half] + both[2 * half :]
    else:
        cut = up_refs[0].shape[2]
        for kt, up_ref in enumerate(up_refs):
            for kf in range(up_ref.shape[0]):
                both = dot(low, up_ref[kf])
                column = (place ^ kf) * sets + ((me ^ kt) & (sets - 1))
                start = pl.multiple_of(column * cut, cut)
                extra_ref[:, pl.ds(start, cut)] = both[: 2 * half] + both[2 * half :]
    first = 0
    for keep_ref, got_ref in zip(keep_refs, got_refs):
        lanes = slice(first, first + keep_ref.shape[1])
        first += keep_ref.shape[1]
        total = keep_ref[...] + got_ref[...].astype(F32) + extra_ref[:, lanes]
        own_ref[:, lanes] = total[:half]
        send_ref[:, lanes] = total[half:].astype(BF16)


def finish_kernel(far_ref, far_got_ref, near_ref, near_got_ref, out_ref, *, own, steps, strips):
    top = lax.axis_index("tensor") >> (log2(lax.axis_size("tensor")) - 1)
    wide = near_ref.shape[1] // strips
    for keep_ref, got_ref, half in ((near_ref, near_got_ref, top), (far_ref, far_got_ref, 1 - top)):
        for i in range(strips):
            lanes = slice(i * wide, (i + 1) * wide)
            total = (keep_ref[:, lanes] + got_ref[:, lanes].astype(F32)).astype(BF16)
            start = pl.multiple_of((2 * i + half) * wide, wide)
            for r in range(own):
                out_ref[:, r, pl.ds(start, wide)] = total[r * steps : (r + 1) * steps]


def shards(queries, cache, new, lengths, weight, down, up):
    parts, spread = lax.axis_size("tensor"), lax.axis_size("fsdp")
    steps, rows, width = queries.shape
    own = rows // parts
    tall = own * steps
    depth, slot = down.shape
    cut = up.shape[1]
    heads, pieces = width // HEAD_DIM, new.shape[2] // HEAD_DIM
    sets = parts // 2
    wide = sets * cut
    half_width = spread * wide
    swap = lambda x, axis, k: lax.ppermute(
        x, axis, [(i, i ^ k) for i in range(lax.axis_size(axis))]
    )

    block = shape_of((own * heads * steps + pieces * tall, HEAD_DIM), BF16)
    per = depth // cut
    sources = (queries, new, down.T, up)
    *blocks, factors = call(
        functools.partial(pack_kernel, parts=parts, own=own, steps=steps),
        "pack",
        [(ANY, a) for a in sources],
        [block] * parts + [shape_of((slot + RANK // per, depth), BF16)],
        [pltpu.VMEM(a.shape, BF16) for a in sources] + [pltpu.SemaphoreType.DMA((4,))],
    )
    got = {k: swap(blocks[k], "tensor", k) for k in range(parts - 1, 0, -1)}
    blocks = [blocks[0]] + [got[k] for k in range(1, parts)]
    factors, blocks[1] = lax.optimization_barrier((factors, blocks[1]))
    factors = [factors] + [swap(factors, "fsdp", k) for k in range(1, spread)]

    strip = pltpu.VMEM((depth, wide), BF16)
    early = spread // 2
    attended, fetched = None, None
    outs = call(
        functools.partial(attend_kernel, parts=parts, own=own, steps=steps, strips=early),
        "attend",
        [(ANY, lengths)] + [(VMEM, b) for b in blocks] + [(ANY, cache), (ANY, weight)],
        [shape_of((tall, width), BF16)] * parts + [strip] * early,
        [
            pltpu.VMEM(cache.shape, BF16),
            pltpu.SMEM(lengths.shape, jnp.int32),
            pltpu.VMEM((parts,) + block.shape, BF16),
            pltpu.VMEM((parts, tall, width), F32),
            pltpu.SemaphoreType.DMA((own, KV_HEADS // 2, 2)),
            pltpu.SemaphoreType.DMA((early + 1,)),
        ],
    )
    attended, far_strips = outs[:parts], outs[parts:]
    far_strips += call(
        functools.partial(fetch_kernel, first=early),
        "fetch",
        [(ANY, attended[0]), (ANY, weight)],
        [strip] * (spread - early),
        [pltpu.SemaphoreType.DMA((spread - early,))],
        cost=pl.CostEstimate(
            flops=0, bytes_accessed=2 * (spread - early) * depth * wide, transcendentals=0
        ),
    )
    got = {k: swap(attended[k], "tensor", k) for k in range(parts - 1, 0, -1)}
    attended = [attended[0]] + [got[k] for k in range(1, parts)]

    down_rows, ups = call(
        functools.partial(collect_kernel, slot=slot),
        "collect",
        [(VMEM, f) for f in factors],
        [shape_of((RANK, depth), BF16), shape_of((spread, RANK, cut), BF16)],
    )
    ordered = cut % HEAD_DIM != 0
    if ordered:
        ups = lax.all_gather(up, ("fsdp", "tensor"), axis=1, tiled=True)
        ups = ups.reshape(RANK, spread, 2, wide)
        top = lax.axis_index("tensor") // sets
        ups = lax.dynamic_index_in_dim(ups, top, 2, keepdims=False)
        up_sets = {0: ups.reshape(RANK, half_width)}
    else:
        up_sets = {0: ups}
        bit = sets // 2
        while bit:
            up_sets |= {k ^ bit: swap(u, "tensor", bit) for k, u in list(up_sets.items())}
            bit //= 2

    order = sorted(range(parts), key=lambda k: format(k, "08b")[::-1])
    attended = [attended[k] for k in order]

    def reduce(keep, send):
        bit = 1
        while True:
            got = swap(send, "tensor", bit)
            bit *= 2
            if bit == sets:
                return keep, got
            both = keep + got.astype(F32)
            half = both.shape[0] // 2
            keep, send = both[:half], both[half:].astype(BF16)

    def reduce_low(keep, send):
        bit = 1
        while True:
            both = fold_low(keep, swap(send, "tensor", bit))
            bit *= 2
            if bit == sets:
                return both
            half = both.shape[0] // 2
            keep, send = both[:half], jnp.concatenate(split(both[half:]), axis=1)

    near = spread // 2
    middle = spread // 4
    keep, send, low_keep, low_send, *near_strips = project(
        attended, far_strips, weight, wide, ahead=near, down=down_rows
    )
    far_keep, far_got = reduce(keep, send)
    low = reduce_low(low_keep, low_send)
    keep_a, send_a, *later_strips = project(
        attended, near_strips, weight, wide, ahead=middle, first=near
    )
    keep_a, got_a = reduce(keep_a, send_a)
    keep_b, send_b = project(
        attended, later_strips, weight, wide, late=spread - near - middle, first=near + middle
    )
    keep_b, got_b = reduce(keep_b, send_b)

    far = far_keep + far_got.astype(F32)
    low_parts = jnp.concatenate(split(low), axis=1)
    message = jnp.concatenate([far[tall:].astype(BF16), low_parts[tall:], low_parts[:tall]], axis=1)
    message = swap(message, "tensor", sets)
    near_got, low_got = message[:, :half_width], message[:, half_width:]

    ups = [up_sets[k] for k in range(len(up_sets))]
    near_keep, near_send = call(
        functools.partial(adapt_kernel, pieces=2, sets=len(ups), ordered=ordered),
        "adapt",
        [(VMEM, a) for a in (low, low_got, keep_a, keep_b, got_a, got_b, *ups)],
        [shape_of((tall, half_width), F32), shape_of((tall, half_width), BF16)],
        [pltpu.VMEM((2 * tall, half_width), F32)],
    )
    far_got = swap(near_send, "tensor", sets)

    return call(
        functools.partial(finish_kernel, own=own, steps=steps, strips=spread),
        "finish",
        [(VMEM, a) for a in (far[:tall], far_got, near_keep, near_got)],
        [shape_of((steps, own, weight.shape[1]), BF16)],
    )[0]


def solution(mesh):
    return jax.shard_map(
        shards,
        mesh=mesh,
        in_specs=(
            P(None, ("groups", "fsdp"), "tensor"),
            P(("groups", "fsdp", "tensor"), None, None, None, None),
            P(None, ("groups", "fsdp"), "tensor"),
            P(("groups", "fsdp", "tensor")),
            P("tensor", None),
            P("tensor", "fsdp"),
            P(None, ("fsdp", "tensor")),
        ),
        out_specs=P(None, ("groups", "fsdp", "tensor"), None),
        check_vma=False,
    )
```

```python
import functools

import jax
import jax.numpy as jnp
from jax import lax
from jax.experimental import pallas as pl
from jax.experimental.pallas import tpu as pltpu
from jax.sharding import PartitionSpec as P

HEADS = 64
KV_HEADS = 8
HEAD_DIM = 128
GROUP = HEADS // KV_HEADS
RANK = 64
LOG2_E = 1.4426950408889634
SCALE = 2.0
BF16 = jnp.bfloat16
F32 = jnp.float32
VMEM = pl.BlockSpec(memory_space=pltpu.VMEM)
ANY = pl.BlockSpec(memory_space=pl.ANY)
HBM = pl.BlockSpec(memory_space=pltpu.HBM)
ROW_ROW = (((1,), (1,)), ((), ()))
shape_of = jax.ShapeDtypeStruct


def dot(a, b):
    return jnp.dot(a, b, preferred_element_type=F32)


def dot_rows(a, b):
    return lax.dot_general(a, b, ROW_ROW, preferred_element_type=F32)


def call(kernel, name, ins, outs, scratch=(), mib=6, cost=None, alias=None):
    specs, args = zip(*ins)
    args = [
        pltpu.with_memory_space_constraint(a, pltpu.HBM) if s is HBM else a for s, a in ins
    ]
    return pl.pallas_call(
        kernel,
        in_specs=list(specs),
        out_specs=[VMEM] * len(outs),
        out_shape=list(outs),
        scratch_shapes=list(scratch),
        input_output_aliases=alias or {},
        compiler_params=pltpu.CompilerParams(vmem_limit_bytes=mib * 2**20),
        cost_estimate=cost,
        name=name,
    )(*args)


def split(x):
    high = x.astype(BF16)
    return high, (x - high.astype(F32)).astype(BF16)


def log2(n):
    return n.bit_length() - 1


def strip_copies(weight_hbm, strips_ref, sem, first):
    count, _, wide = strips_ref.shape
    spread = weight_hbm.shape[1] // (2 * wide)
    top = lax.axis_index("tensor") >> (log2(lax.axis_size("tensor")) - 1)
    copies = []
    for i in range(count):
        half = top if first + i >= spread else 1 - top
        start = pl.multiple_of((2 * ((first + i) % spread) + half) * wide, wide)
        copies.append(
            pltpu.make_async_copy(
                weight_hbm.at[:, pl.ds(start, wide)], strips_ref.at[i], sem.at[i]
            )
        )
    return copies


def pack_kernel(query_hbm, new_hbm, *refs, parts, own, steps):
    *block_refs, query_ref, new_ref, sem = refs
    copies = [
        pltpu.make_async_copy(query_hbm, query_ref, sem.at[0]),
        pltpu.make_async_copy(new_hbm, new_ref, sem.at[1]),
    ]
    for copy in copies:
        copy.start()
    me = lax.axis_index("tensor")
    count = steps * parts * own
    i = lax.broadcasted_iota(jnp.int32, (count, count), 0)
    j = lax.broadcasted_iota(jnp.int32, (count, count), 1)
    step_out = i & (steps - 1)
    row_out = (i >> log2(steps)) & (own - 1)
    part_out = (i >> log2(steps * own)) ^ me
    source = step_out * (parts * own) + part_out * own + row_out
    select = jnp.where(source == j, 1.0, 0.0).astype(BF16)
    for copy in copies:
        copy.wait()
    queries = dot(select, query_ref[...].reshape(count, query_ref.shape[2]))
    new = dot(select, new_ref[...].reshape(count, new_ref.shape[2]))
    heads = queries.shape[1] // HEAD_DIM
    pieces = new.shape[1] // HEAD_DIM
    tall = own * steps
    for k in range(parts):
        q = queries[k * tall : (k + 1) * tall]
        n = new[k * tall : (k + 1) * tall]
        tiles = [
            q[r * steps : (r + 1) * steps, h * HEAD_DIM : (h + 1) * HEAD_DIM]
            for r in range(own)
            for h in range(heads)
        ]
        tiles += [n[:, c * HEAD_DIM : (c + 1) * HEAD_DIM] for c in range(pieces)]
        block = jnp.concatenate(tiles, axis=0).astype(BF16)
        if k < parts // 2:
            block_refs[k][...] = block
        else:
            block_refs[-1][k - parts // 2] = block


def stage_kernel(after_ref, cache_hbm, down_hbm, up_hbm, cache_ref, factor_ref, up_ref, sem):
    slot, depth = down_hbm.shape
    copies = [
        pltpu.make_async_copy(up_hbm, up_ref, sem.at[0]),
        pltpu.make_async_copy(down_hbm, factor_ref.at[pl.ds(0, slot)], sem.at[1]),
    ]
    slots = pl.ds(0, cache_hbm.shape[3])
    for r in range(cache_hbm.shape[0]):
        for part in range(2):
            copies.append(
                pltpu.make_async_copy(
                    cache_hbm.at[r, part],
                    cache_ref.at[r, part, :, slots],
                    sem.at[2 + 2 * r + part],
                )
            )
    for copy in copies:
        copy.start()
    cut = up_ref.shape[1]
    per = depth // cut
    tall = RANK // per
    copies[0].wait()
    for c in range(per):
        factor_ref[slot : slot + tall, c * cut : (c + 1) * cut] = up_ref[c * tall : (c + 1) * tall, :]
    for copy in copies[1:]:
        copy.wait()


def attend_kernel(length_hbm, *refs, parts, own, steps):
    block_refs, refs = refs[:parts], refs[parts:]
    weight_hbm, refs = refs[0], refs[2:]
    out_refs, refs = refs[:parts], refs[parts:]
    strips_ref, cache_ref, length_ref, held_ref, attended_ref = refs[:5]
    scores_ref, weights_ref, length_sem, sem = refs[5:]
    length_copy = pltpu.make_async_copy(length_hbm, length_ref, length_sem)
    length_copy.start()
    heads = HEADS // parts
    pieces = 2 * KV_HEADS // parts
    query_rows = own * heads * steps
    tall = own * steps
    slots = cache_ref.shape[3] - tall
    count = GROUP * steps
    turns = own * KV_HEADS
    weight_copies = strip_copies(weight_hbm, strips_ref, sem, 0)
    for copy in weight_copies:
        copy.start()

    me = lax.axis_index("tensor")
    for k, block_ref in enumerate(block_refs):
        held_ref[me ^ k] = block_ref[0:query_rows, :]
        for c in range(pieces):
            piece = (me ^ k) * pieces + c
            start = query_rows + c * tall
            for r in range(own):
                cache_ref[r, piece >> log2(KV_HEADS), piece & (KV_HEADS - 1), slots : slots + tall, :] = (
                    block_ref[start : start + tall, :]
                )

    def queries(r, g):
        if heads >= GROUP:
            groups = heads // GROUP
            start = (r * heads + (g & (groups - 1)) * GROUP) * steps
            return held_ref[g >> log2(groups), pl.ds(pl.multiple_of(start, count), count), :]
        span = GROUP // heads
        start = pl.multiple_of(r * heads * steps, heads * steps)
        found = [held_ref[g * span + i, pl.ds(start, heads * steps), :] for i in range(span)]
        return jnp.concatenate(found, axis=0)

    slot = lax.broadcasted_iota(jnp.int32, (count, slots + tall), 1)
    step = lax.broadcasted_iota(jnp.int32, (count, slots + tall), 0) & (steps - 1)
    ones = jnp.ones((slots + tall, HEAD_DIM), BF16)
    length_copy.wait()

    def turn(j, _):
        scored = jnp.minimum(j, turns - 1)
        r, g = scored >> log2(KV_HEADS), scored & (KV_HEADS - 1)
        summed = jnp.maximum(j - 2, 0)
        r_out, g_out = summed >> log2(KV_HEADS), summed & (KV_HEADS - 1)

        fresh = slot - slots - r * steps
        valid = (slot < length_ref[r]) | ((fresh >= 0) & (fresh <= step))
        scores = dot_rows(queries(r, g), cache_ref[r, 0, g]) * (HEAD_DIM**-0.5 * LOG2_E)
        before = scores_ref[(j + 1) & 1]
        weights = jnp.exp2(before - before.max(-1, keepdims=True))
        values = jnp.concatenate([cache_ref[r_out, 1, g_out], ones], axis=1)
        mixed = dot(weights_ref[j & 1], values)
        mixed = mixed[:count] + mixed[count:]
        mixed = mixed[:, :HEAD_DIM] / mixed[:, HEAD_DIM:]

        high, rest = split(weights)
        weights_ref[(j + 1) & 1, 0:count, :] = high
        weights_ref[(j + 1) & 1, count : 2 * count, :] = rest
        scores_ref[j & 1] = jnp.where(valid, scores, -1e30)
        row = pl.ds(pl.multiple_of(r_out * steps, steps), steps)
        for h in range(GROUP):
            head = g_out * GROUP + h
            attended_ref[head >> log2(heads), head & (heads - 1), row, :] = mixed[
                h * steps : (h + 1) * steps
            ]
        return 0

    lax.fori_loop(0, turns + 2, turn, 0, unroll=2)
    for k in range(parts):
        for h in range(heads):
            out_refs[k][:, h * HEAD_DIM : (h + 1) * HEAD_DIM] = attended_ref[me ^ k, h].astype(BF16)
    for copy in weight_copies:
        copy.wait()


def collect_kernel(*refs, slot):
    _, *factor_refs, down_ref, up_ref = refs
    me = lax.axis_index("fsdp")
    cut = up_ref.shape[2]
    per = down_ref.shape[1] // cut
    tall = RANK // per
    for k, factor_ref in enumerate(factor_refs):
        down_ref[pl.ds(pl.multiple_of((me ^ k) * slot, slot), slot), :] = factor_ref[0:slot, :]
        for c in range(per):
            up_ref[k, c * tall : (c + 1) * tall, :] = factor_ref[
                slot : slot + tall, c * cut : (c + 1) * cut
            ]


def fetch_kernel(after_ref, weight_hbm, strips_ref, sem, *, first):
    copies = strip_copies(weight_hbm, strips_ref, sem, first)
    for copy in copies:
        copy.start()
    for copy in copies:
        copy.wait()


def project_kernel(*refs, parts, spans, ahead, first):
    attended_refs, refs = refs[:parts], refs[parts:]
    held_refs, refs = refs[: len(spans)], refs[len(spans) :]
    weight_hbm, keep_ref, send_ref, refs = refs[0], refs[1], refs[2], refs[3:]
    copies = []
    if ahead:
        ahead_ref, rows_ref, sem = refs
        copies = strip_copies(weight_hbm, ahead_ref, sem, first)
    else:
        rows_ref = refs[0]
    for copy in copies:
        copy.start()
    tall = attended_refs[0].shape[0]
    for k, attended_ref in enumerate(attended_refs):
        rows_ref[k * tall : (k + 1) * tall, :] = attended_ref[...]
    half = rows_ref.shape[0] // 2
    place = 0
    for strips_ref, (low, high) in zip(held_refs, spans):
        wide = strips_ref.shape[2]

        @pl.loop(low, high)
        def _(i, strips_ref=strips_ref, place=place - low):
            out = dot(rows_ref[...], strips_ref[i])
            lanes = pl.ds(pl.multiple_of((place + i) * wide, wide), wide)
            keep_ref[:, lanes] = out[:half]
            send_ref[:, lanes] = out[half:].astype(BF16)

        place += high - low
    for copy in copies:
        copy.wait()


def project(attended, weight, buffers, low, high, ahead=0):
    parts = len(attended)
    tall, depth = attended[0].shape
    half = parts * tall // 2
    held, spans = [], []
    for first, buffer in buffers:
        a, b = max(low - first, 0), min(high - first, buffer.shape[0])
        if a < b:
            held.append(buffer)
            spans.append((a, b))
    wide = held[0].shape[2]
    width = wide * (high - low)
    next_strip = buffers[-1][0] + buffers[-1][1].shape[0]
    outs = [shape_of((half, width), F32), shape_of((half, width), BF16)]
    ins = [(VMEM, a) for a in attended] + [(VMEM, h) for h in held] + [(HBM, weight)]
    scratch = [pltpu.VMEM((parts * tall, depth), BF16)]
    if ahead:
        outs += [pltpu.VMEM((ahead, depth, wide), BF16)]
        scratch += [pltpu.SemaphoreType.DMA((ahead,))]
    kernel = functools.partial(
        project_kernel, parts=parts, spans=spans, ahead=ahead, first=next_strip
    )
    cost = pl.CostEstimate(
        flops=2 * parts * tall * depth * width, bytes_accessed=2 * depth * width, transcendentals=0
    )
    keep, send, *rest = call(kernel, "project", ins, outs, scratch, cost=cost)
    return keep, send, buffers + [(next_strip, rest[0])] if ahead else buffers


def lower_kernel(*refs):
    *attended_refs, down_ref, keep_ref, send_ref = refs
    half = len(attended_refs) // 2
    for first, last in ((0, half), (half, 2 * half)):
        rows = jnp.concatenate([a[...] for a in attended_refs[first:last]], axis=0)
        low = dot_rows(rows, down_ref[...])
        if first:
            send_ref[...] = jnp.concatenate(split(low), axis=1)
        else:
            keep_ref[...] = low


def fold_low(keep, got):
    return keep + got[:, :RANK].astype(F32) + got[:, RANK:].astype(F32)


def adapt_kernel(*refs, pieces, sets, ordered):
    low_ref, low_got_ref, refs = refs[0], refs[1], refs[2:]
    keep_refs, refs = refs[:pieces], refs[pieces:]
    got_refs, refs = refs[:pieces], refs[pieces:]
    up_refs, (own_ref, send_ref, extra_ref) = refs[:sets], refs[sets:]
    me, place = lax.axis_index("tensor"), lax.axis_index("fsdp")
    half = low_ref.shape[0] // 2
    got = low_got_ref[...]
    got = jnp.concatenate([got[:, : 2 * RANK], got[:, 2 * RANK :]], axis=0)
    low = SCALE * fold_low(low_ref[...], got)
    low = jnp.concatenate(split(low), axis=0)
    if ordered:
        both = dot(low, up_refs[0][...])
        extra_ref[...] = both[: 2 * half] + both[2 * half :]
    else:
        cut = up_refs[0].shape[2]
        for kt, up_ref in enumerate(up_refs):
            for kf in range(up_ref.shape[0]):
                both = dot(low, up_ref[kf])
                column = (place ^ kf) * sets + ((me ^ kt) & (sets - 1))
                start = pl.multiple_of(column * cut, cut)
                extra_ref[:, pl.ds(start, cut)] = both[: 2 * half] + both[2 * half :]
    first = 0
    for keep_ref, got_ref in zip(keep_refs, got_refs):
        lanes = slice(first, first + keep_ref.shape[1])
        first += keep_ref.shape[1]
        total = keep_ref[...] + got_ref[...].astype(F32) + extra_ref[:, lanes]
        own_ref[:, lanes] = total[:half]
        send_ref[:, lanes] = total[half:].astype(BF16)


def finish_kernel(far_ref, far_got_ref, near_ref, near_got_ref, out_ref, *, own, steps, strips):
    top = lax.axis_index("tensor") >> (log2(lax.axis_size("tensor")) - 1)
    wide = near_ref.shape[1] // strips
    for keep_ref, got_ref, half in ((near_ref, near_got_ref, top), (far_ref, far_got_ref, 1 - top)):
        for i in range(strips):
            lanes = slice(i * wide, (i + 1) * wide)
            total = (keep_ref[:, lanes] + got_ref[:, lanes].astype(F32)).astype(BF16)
            start = pl.multiple_of((2 * i + half) * wide, wide)
            for r in range(own):
                out_ref[:, r, pl.ds(start, wide)] = total[r * steps : (r + 1) * steps]


def shards(queries, cache, new, lengths, weight, down, up):
    parts, spread = lax.axis_size("tensor"), lax.axis_size("fsdp")
    steps, rows, width = queries.shape
    own = rows // parts
    tall = own * steps
    depth, slot = down.shape
    cut = up.shape[1]
    heads, pieces = width // HEAD_DIM, new.shape[2] // HEAD_DIM
    sets = parts // 2
    wide = sets * cut
    half_width = spread * wide
    swap = lambda x, axis, k: lax.ppermute(
        x, axis, [(i, i ^ k) for i in range(lax.axis_size(axis))]
    )

    block = shape_of((own * heads * steps + pieces * tall, HEAD_DIM), BF16)
    per = depth // cut
    *blocks, cross = call(
        functools.partial(pack_kernel, parts=parts, own=own, steps=steps),
        "pack",
        [(HBM, queries), (HBM, new)],
        [block] * sets + [shape_of((sets,) + block.shape, BF16)],
        [pltpu.VMEM(queries.shape, BF16), pltpu.VMEM(new.shape, BF16), pltpu.SemaphoreType.DMA((2,))],
    )
    cache, factors = call(
        stage_kernel,
        "stage",
        [(ANY, blocks[0]), (HBM, cache), (HBM, down.T), (HBM, up)],
        [
            pltpu.VMEM(cache.shape[:3] + (cache.shape[3] + tall, HEAD_DIM), BF16),
            shape_of((slot + RANK // per, depth), BF16),
        ],
        [pltpu.VMEM(up.shape, BF16), pltpu.SemaphoreType.DMA((2 + 2 * own,))],
        cost=pl.CostEstimate(flops=0, bytes_accessed=2 * cache.size, transcendentals=0),
    )
    cross = swap(cross, "tensor", sets)
    blocks = blocks[:1] + [swap(blocks[k], "tensor", k) for k in range(1, sets)]
    blocks += [cross[0]] + [swap(cross[k], "tensor", k) for k in range(1, sets)]
    factors = {0: factors}
    bit = spread // 2
    while bit > 1:
        factors |= {k ^ bit: swap(v, "fsdp", bit) for k, v in list(factors.items())}
        bit //= 2
    near_factors, blocks[sets] = lax.optimization_barrier((factors[0], blocks[sets]))

    half, quarter = spread // 2, spread // 4
    early = half + quarter
    fetched = quarter
    attended = call(
        functools.partial(attend_kernel, parts=parts, own=own, steps=steps),
        "attend",
        [(HBM, lengths)] + [(VMEM, b) for b in blocks] + [(HBM, weight), (VMEM, cache)],
        [shape_of((tall, width), BF16)] * parts
        + [pltpu.VMEM((early, depth, wide), BF16), pltpu.VMEM(cache.shape, BF16)],
        [
            pltpu.SMEM(lengths.shape, jnp.int32),
            pltpu.VMEM((parts, own * heads * steps, HEAD_DIM), BF16),
            pltpu.VMEM((parts, heads, tall, HEAD_DIM), F32),
            pltpu.VMEM((2, GROUP * steps, cache.shape[3]), F32),
            pltpu.VMEM((2, 2 * GROUP * steps, cache.shape[3]), BF16),
            pltpu.SemaphoreType.DMA(()),
            pltpu.SemaphoreType.DMA((early,)),
        ],
        alias={parts + 2: parts + 1},
    )
    attended, buffers = attended[:parts], [(0, attended[parts])]
    buffers += [
        (
            early,
            call(
                functools.partial(fetch_kernel, first=early),
                "fetch",
                [(ANY, attended[0]), (HBM, weight)],
                [pltpu.VMEM((fetched, depth, wide), BF16)],
                [pltpu.SemaphoreType.DMA((fetched,))],
                cost=pl.CostEstimate(
                    flops=0, bytes_accessed=2 * fetched * depth * wide, transcendentals=0
                ),
            )[0],
        )
    ]
    factors[1] = swap(near_factors, "fsdp", 1)
    attended, factors = lax.optimization_barrier((list(attended), factors))
    factors |= {k ^ 1: swap(v, "fsdp", 1) for k, v in list(factors.items()) if k > 1}
    got = {k: swap(attended[k], "tensor", k) for k in range(parts - 1, 0, -1)}
    attended = [attended[0]] + [got[k] for k in range(1, parts)]

    order = sorted(range(parts), key=lambda k: format(k, "08b")[::-1])
    attended = [attended[k] for k in order]

    def reduce(keep, send):
        bit = 1
        while True:
            got = swap(send, "tensor", bit)
            bit *= 2
            if bit == sets:
                return keep, got
            both = keep + got.astype(F32)
            half = both.shape[0] // 2
            keep, send = both[:half], both[half:].astype(BF16)

    def reduce_low(keep, send):
        bit = 1
        while True:
            both = fold_low(keep, swap(send, "tensor", bit))
            bit *= 2
            if bit == sets:
                return both
            half = both.shape[0] // 2
            keep, send = both[:half], jnp.concatenate(split(both[half:]), axis=1)

    keep, send, buffers = project(attended, weight, buffers, 0, spread, half)
    far_keep, far_got = reduce(keep, send)

    down_rows, ups = call(
        functools.partial(collect_kernel, slot=slot),
        "collect",
        [(ANY, keep)] + [(VMEM, factors[k]) for k in range(spread)],
        [shape_of((RANK, depth), BF16), shape_of((spread, RANK, cut), BF16)],
    )
    low_keep, low_send = call(
        lower_kernel,
        "lower",
        [(VMEM, a) for a in (*attended, down_rows)],
        [shape_of((sets * tall, RANK), F32), shape_of((sets * tall, 2 * RANK), BF16)],
    )
    low = reduce_low(low_keep, low_send)
    ordered = cut % HEAD_DIM != 0
    if ordered:
        ups = lax.all_gather(up, ("fsdp", "tensor"), axis=1, tiled=True)
        ups = ups.reshape(RANK, spread, 2, wide)
        top = lax.axis_index("tensor") // sets
        ups = lax.dynamic_index_in_dim(ups, top, 2, keepdims=False)
        up_sets = {0: ups.reshape(RANK, half_width)}
    else:
        up_sets = {0: ups}
        bit = sets // 2
        while bit:
            up_sets |= {k ^ bit: swap(u, "tensor", bit) for k, u in list(up_sets.items())}
            bit //= 2

    middle = spread + half
    keep_a, send_a, buffers = project(attended, weight, buffers, spread, middle, half)
    keep_a, got_a = reduce(keep_a, send_a)
    keep_b, send_b, _ = project(attended, weight, buffers, middle, 2 * spread)
    keep_b, got_b = reduce(keep_b, send_b)

    far = far_keep + far_got.astype(F32)
    low_parts = jnp.concatenate(split(low), axis=1)
    message = jnp.concatenate([far[tall:].astype(BF16), low_parts[tall:], low_parts[:tall]], axis=1)
    message = swap(message, "tensor", sets)
    near_got, low_got = message[:, :half_width], message[:, half_width:]

    ups = [up_sets[k] for k in range(len(up_sets))]
    near_keep, near_send = call(
        functools.partial(adapt_kernel, pieces=2, sets=len(ups), ordered=ordered),
        "adapt",
        [(VMEM, a) for a in (low, low_got, keep_a, keep_b, got_a, got_b, *ups)],
        [shape_of((tall, half_width), F32), shape_of((tall, half_width), BF16)],
        [pltpu.VMEM((2 * tall, half_width), F32)],
    )
    far_got = swap(near_send, "tensor", sets)

    return call(
        functools.partial(finish_kernel, own=own, steps=steps, strips=spread),
        "finish",
        [(VMEM, a) for a in (far[:tall], far_got, near_keep, near_got)],
        [shape_of((steps, own, weight.shape[1]), BF16)],
    )[0]


def solution(mesh):
    return jax.shard_map(
        shards,
        mesh=mesh,
        in_specs=(
            P(None, ("groups", "fsdp"), "tensor"),
            P(("groups", "fsdp", "tensor"), None, None, None, None),
            P(None, ("groups", "fsdp"), "tensor"),
            P(("groups", "fsdp", "tensor")),
            P("tensor", None),
            P("tensor", "fsdp"),
            P(None, ("fsdp", "tensor")),
        ),
        out_specs=P(None, ("groups", "fsdp", "tensor"), None),
        check_vma=False,
    )
```

```python
import functools

import jax
import jax.numpy as jnp
from jax import lax
from jax.experimental import pallas as pl
from jax.experimental.pallas import tpu as pltpu
from jax.sharding import PartitionSpec as P

HEADS = 64
KV_HEADS = 8
HEAD_DIM = 128
GROUP = HEADS // KV_HEADS
RANK = 64
LOG2_E = 1.4426950408889634
SCALE = 2.0
BF16 = jnp.bfloat16
F32 = jnp.float32
VMEM = pl.BlockSpec(memory_space=pltpu.VMEM)
ANY = pl.BlockSpec(memory_space=pl.ANY)
HBM = pl.BlockSpec(memory_space=pltpu.HBM)
ROW_ROW = (((1,), (1,)), ((), ()))
shape_of = jax.ShapeDtypeStruct


def dot(a, b):
    return jnp.dot(a, b, preferred_element_type=F32)


def dot_rows(a, b):
    return lax.dot_general(a, b, ROW_ROW, preferred_element_type=F32)


def call(kernel, name, ins, outs, scratch=(), mib=6, cost=None, alias=None):
    specs, args = zip(*ins)
    args = [
        pltpu.with_memory_space_constraint(a, pltpu.HBM) if s is HBM else a for s, a in ins
    ]
    return pl.pallas_call(
        kernel,
        in_specs=list(specs),
        out_specs=[VMEM] * len(outs),
        out_shape=list(outs),
        scratch_shapes=list(scratch),
        input_output_aliases=alias or {},
        compiler_params=pltpu.CompilerParams(vmem_limit_bytes=mib * 2**20),
        cost_estimate=cost,
        name=name,
    )(*args)


def split(x):
    high = x.astype(BF16)
    return high, (x - high.astype(F32)).astype(BF16)


def log2(n):
    return n.bit_length() - 1


def strip_copies(weight_hbm, strips_ref, sem, first):
    count, _, wide = strips_ref.shape
    spread = weight_hbm.shape[1] // (2 * wide)
    top = lax.axis_index("tensor") >> (log2(lax.axis_size("tensor")) - 1)
    copies = []
    for i in range(count):
        half = top if first + i >= spread else 1 - top
        start = pl.multiple_of((2 * ((first + i) % spread) + half) * wide, wide)
        copies.append(
            pltpu.make_async_copy(
                weight_hbm.at[:, pl.ds(start, wide)], strips_ref.at[i], sem.at[i]
            )
        )
    return copies


def pack_kernel(query_hbm, new_hbm, cache_hbm, down_hbm, up_hbm, *refs, parts, own, steps):
    *block_refs, cache_ref, factor_ref, query_ref, new_ref, up_ref, sem = refs
    slot, depth = down_hbm.shape
    pairs = [
        (query_hbm, query_ref),
        (new_hbm, new_ref),
        (up_hbm, up_ref),
        (down_hbm, factor_ref.at[pl.ds(0, slot)]),
    ]
    slots = pl.ds(0, cache_hbm.shape[3])
    pairs += [
        (cache_hbm.at[r, part], cache_ref.at[r, part, :, slots])
        for r in range(own)
        for part in range(2)
    ]
    copies = [pltpu.make_async_copy(*pair, sem.at[i]) for i, pair in enumerate(pairs)]
    for copy in copies:
        copy.start()
    me = lax.axis_index("tensor")
    count = steps * parts * own
    i = lax.broadcasted_iota(jnp.int32, (count, count), 0)
    j = lax.broadcasted_iota(jnp.int32, (count, count), 1)
    step_out = i & (steps - 1)
    row_out = (i >> log2(steps)) & (own - 1)
    part_out = (i >> log2(steps * own)) ^ me
    source = step_out * (parts * own) + part_out * own + row_out
    select = jnp.where(source == j, 1.0, 0.0).astype(BF16)
    for copy in copies[:3]:
        copy.wait()
    queries = dot(select, query_ref[...].reshape(count, query_ref.shape[2]))
    new = dot(select, new_ref[...].reshape(count, new_ref.shape[2]))
    heads = queries.shape[1] // HEAD_DIM
    pieces = new.shape[1] // HEAD_DIM
    tall = own * steps
    for k in range(parts):
        q = queries[k * tall : (k + 1) * tall]
        n = new[k * tall : (k + 1) * tall]
        tiles = [
            q[r * steps : (r + 1) * steps, h * HEAD_DIM : (h + 1) * HEAD_DIM]
            for r in range(own)
            for h in range(heads)
        ]
        tiles += [n[:, c * HEAD_DIM : (c + 1) * HEAD_DIM] for c in range(pieces)]
        block = jnp.concatenate(tiles, axis=0).astype(BF16)
        if k < parts // 2:
            block_refs[k][...] = block
        else:
            block_refs[-1][k - parts // 2] = block
    cut = up_ref.shape[1]
    per = depth // cut
    tall = RANK // per
    for c in range(per):
        factor_ref[slot : slot + tall, c * cut : (c + 1) * cut] = up_ref[c * tall : (c + 1) * tall, :]
    for copy in copies[3:]:
        copy.wait()


def attend_kernel(length_hbm, *refs, parts, own, steps):
    block_refs, refs = refs[:parts], refs[parts:]
    weight_hbm, refs = refs[0], refs[2:]
    out_refs, refs = refs[:parts], refs[parts:]
    strips_ref, cache_ref, length_ref, held_ref, attended_ref = refs[:5]
    scores_ref, weights_ref, mask_ref, length_sem, sem = refs[5:]
    length_copy = pltpu.make_async_copy(length_hbm, length_ref, length_sem)
    length_copy.start()
    heads = HEADS // parts
    pieces = 2 * KV_HEADS // parts
    query_rows = own * heads * steps
    tall = own * steps
    slots = cache_ref.shape[3] - tall
    count = GROUP * steps
    weight_copies = strip_copies(weight_hbm, strips_ref, sem, 0)
    for copy in weight_copies:
        copy.start()

    me = lax.axis_index("tensor")
    for k, block_ref in enumerate(block_refs):
        held_ref[me ^ k] = block_ref[0:query_rows, :]
        for c in range(pieces):
            piece = (me ^ k) * pieces + c
            start = query_rows + c * tall
            for r in range(own):
                cache_ref[r, piece >> log2(KV_HEADS), piece & (KV_HEADS - 1), slots : slots + tall, :] = (
                    block_ref[start : start + tall, :]
                )

    def queries(r, g):
        if heads >= GROUP:
            groups = heads // GROUP
            start = (r * heads + (g & (groups - 1)) * GROUP) * steps
            return held_ref[g >> log2(groups), pl.ds(pl.multiple_of(start, count), count), :]
        span = GROUP // heads
        start = pl.multiple_of(r * heads * steps, heads * steps)
        found = [held_ref[g * span + i, pl.ds(start, heads * steps), :] for i in range(span)]
        return jnp.concatenate(found, axis=0)

    slot = lax.broadcasted_iota(jnp.int32, (count, slots + tall), 1)
    step = lax.broadcasted_iota(jnp.int32, (count, slots + tall), 0) & (steps - 1)
    length_copy.wait()
    for r in range(own):
        fresh = slot - slots - r * steps
        valid = (slot < length_ref[r]) | ((fresh >= 0) & (fresh <= step))
        mask_ref[r] = jnp.where(valid, 0.0, -1e30)
    ones = jnp.ones((slots + tall, HEAD_DIM), BF16)

    def turn(i, _):
        scored = jnp.minimum(i, KV_HEADS - 1)
        summed = jnp.maximum(i - 2, 0)
        rows = range(own)
        mixed = [
            dot(weights_ref[r], jnp.concatenate([cache_ref[r, 1, summed], ones], axis=1)) for r in rows
        ]
        before = [scores_ref[r] for r in rows]
        weights = [jnp.exp2(b - b.max(-1, keepdims=True)) for b in before]
        scores = [
            dot_rows(queries(r, scored), cache_ref[r, 0, scored]) * (HEAD_DIM**-0.5 * LOG2_E)
            + mask_ref[r]
            for r in rows
        ]
        for r in rows:
            weights_ref[r] = jnp.concatenate(split(weights[r]), axis=0)
            scores_ref[r] = scores[r]
            total = mixed[r][:count] + mixed[r][count:]
            total = total[:, :HEAD_DIM] / total[:, HEAD_DIM:]
            for h in range(GROUP):
                head = summed * GROUP + h
                attended_ref[
                    head >> log2(heads), head & (heads - 1), r * steps : (r + 1) * steps, :
                ] = total[h * steps : (h + 1) * steps]
        return 0

    lax.fori_loop(0, KV_HEADS + 2, turn, 0, unroll=2)
    for k in range(parts):
        for h in range(heads):
            out_refs[k][:, h * HEAD_DIM : (h + 1) * HEAD_DIM] = attended_ref[me ^ k, h].astype(BF16)
    for copy in weight_copies:
        copy.wait()


def collect_kernel(*refs, slot):
    _, *factor_refs, down_ref, up_ref = refs
    me = lax.axis_index("fsdp")
    cut = up_ref.shape[2]
    per = down_ref.shape[1] // cut
    tall = RANK // per
    for k, factor_ref in enumerate(factor_refs):
        down_ref[pl.ds(pl.multiple_of((me ^ k) * slot, slot), slot), :] = factor_ref[0:slot, :]
        for c in range(per):
            up_ref[k, c * tall : (c + 1) * tall, :] = factor_ref[
                slot : slot + tall, c * cut : (c + 1) * cut
            ]


def fetch_kernel(after_ref, weight_hbm, strips_ref, sem, *, first):
    copies = strip_copies(weight_hbm, strips_ref, sem, first)
    for copy in copies:
        copy.start()
    for copy in copies:
        copy.wait()


def project_kernel(*refs, parts, spans, ahead, first):
    attended_refs, refs = refs[:parts], refs[parts:]
    held_refs, refs = refs[: len(spans)], refs[len(spans) :]
    weight_hbm, keep_ref, send_ref, refs = refs[0], refs[1], refs[2], refs[3:]
    copies = []
    if ahead:
        ahead_ref, rows_ref, sem = refs
        copies = strip_copies(weight_hbm, ahead_ref, sem, first)
    else:
        rows_ref = refs[0]
    for copy in copies:
        copy.start()
    tall = attended_refs[0].shape[0]
    for k, attended_ref in enumerate(attended_refs):
        rows_ref[k * tall : (k + 1) * tall, :] = attended_ref[...]
    half = rows_ref.shape[0] // 2
    place = 0
    for strips_ref, (low, high) in zip(held_refs, spans):
        wide = strips_ref.shape[2]

        @pl.loop(low, high + jnp.minimum(lax.axis_index("tensor"), 0))
        def _(i, strips_ref=strips_ref, place=place - low):
            out = dot(rows_ref[...], strips_ref[i])
            lanes = pl.ds(pl.multiple_of((place + i) * wide, wide), wide)
            keep_ref[:, lanes] = out[:half]
            send_ref[:, lanes] = out[half:].astype(BF16)

        place += high - low
    for copy in copies:
        copy.wait()


def project(attended, weight, buffers, low, high, ahead=0):
    parts = len(attended)
    tall, depth = attended[0].shape
    half = parts * tall // 2
    held, spans = [], []
    for first, buffer in buffers:
        a, b = max(low - first, 0), min(high - first, buffer.shape[0])
        if a < b:
            held.append(buffer)
            spans.append((a, b))
    wide = held[0].shape[2]
    width = wide * (high - low)
    next_strip = buffers[-1][0] + buffers[-1][1].shape[0]
    outs = [shape_of((half, width), F32), shape_of((half, width), BF16)]
    ins = [(VMEM, a) for a in attended] + [(VMEM, h) for h in held] + [(HBM, weight)]
    scratch = [pltpu.VMEM((parts * tall, depth), BF16)]
    if ahead:
        outs += [pltpu.VMEM((ahead, depth, wide), BF16)]
        scratch += [pltpu.SemaphoreType.DMA((ahead,))]
    kernel = functools.partial(
        project_kernel, parts=parts, spans=spans, ahead=ahead, first=next_strip
    )
    cost = pl.CostEstimate(
        flops=2 * parts * tall * depth * width, bytes_accessed=2 * depth * width, transcendentals=0
    )
    keep, send, *rest = call(kernel, "project", ins, outs, scratch, cost=cost)
    return keep, send, buffers + [(next_strip, rest[0])] if ahead else buffers


def lower_kernel(*refs):
    *attended_refs, down_ref, keep_ref, send_ref = refs
    half = len(attended_refs) // 2
    for first, last in ((0, half), (half, 2 * half)):
        rows = jnp.concatenate([a[...] for a in attended_refs[first:last]], axis=0)
        low = dot_rows(rows, down_ref[...])
        if first:
            send_ref[...] = jnp.concatenate(split(low), axis=1)
        else:
            keep_ref[...] = low


def fold_low(keep, got):
    return keep + got[:, :RANK].astype(F32) + got[:, RANK:].astype(F32)


def adapt_kernel(*refs, pieces, sets, ordered):
    low_ref, low_got_ref, refs = refs[0], refs[1], refs[2:]
    keep_refs, refs = refs[:pieces], refs[pieces:]
    got_refs, refs = refs[:pieces], refs[pieces:]
    up_refs, (own_ref, send_ref, extra_ref) = refs[:sets], refs[sets:]
    me, place = lax.axis_index("tensor"), lax.axis_index("fsdp")
    half = low_ref.shape[0] // 2
    got = low_got_ref[...]
    got = jnp.concatenate([got[:, : 2 * RANK], got[:, 2 * RANK :]], axis=0)
    low = SCALE * fold_low(low_ref[...], got)
    low = jnp.concatenate(split(low), axis=0)
    if ordered:
        both = dot(low, up_refs[0][...])
        extra_ref[...] = both[: 2 * half] + both[2 * half :]
    else:
        cut = up_refs[0].shape[2]
        for kt, up_ref in enumerate(up_refs):
            for kf in range(up_ref.shape[0]):
                both = dot(low, up_ref[kf])
                column = (place ^ kf) * sets + ((me ^ kt) & (sets - 1))
                start = pl.multiple_of(column * cut, cut)
                extra_ref[:, pl.ds(start, cut)] = both[: 2 * half] + both[2 * half :]
    first = 0
    for keep_ref, got_ref in zip(keep_refs, got_refs):
        lanes = slice(first, first + keep_ref.shape[1])
        first += keep_ref.shape[1]
        total = keep_ref[...] + got_ref[...].astype(F32) + extra_ref[:, lanes]
        own_ref[:, lanes] = total[:half]
        send_ref[:, lanes] = total[half:].astype(BF16)


def finish_kernel(far_ref, far_got_ref, near_ref, near_got_ref, out_ref, *, own, steps, strips):
    top = lax.axis_index("tensor") >> (log2(lax.axis_size("tensor")) - 1)
    wide = near_ref.shape[1] // strips
    for keep_ref, got_ref, half in ((near_ref, near_got_ref, top), (far_ref, far_got_ref, 1 - top)):
        for i in range(strips):
            lanes = slice(i * wide, (i + 1) * wide)
            total = (keep_ref[:, lanes] + got_ref[:, lanes].astype(F32)).astype(BF16)
            start = pl.multiple_of((2 * i + half) * wide, wide)
            for r in range(own):
                out_ref[:, r, pl.ds(start, wide)] = total[r * steps : (r + 1) * steps]


def shards(queries, cache, new, lengths, weight, down, up):
    parts, spread = lax.axis_size("tensor"), lax.axis_size("fsdp")
    steps, rows, width = queries.shape
    own = rows // parts
    tall = own * steps
    depth, slot = down.shape
    cut = up.shape[1]
    heads, pieces = width // HEAD_DIM, new.shape[2] // HEAD_DIM
    sets = parts // 2
    wide = sets * cut
    half_width = spread * wide
    swap = lambda x, axis, k: lax.ppermute(
        x, axis, [(i, i ^ k) for i in range(lax.axis_size(axis))]
    )

    block = shape_of((own * heads * steps + pieces * tall, HEAD_DIM), BF16)
    per = depth // cut
    *blocks, cross, cache, factors = call(
        functools.partial(pack_kernel, parts=parts, own=own, steps=steps),
        "pack",
        [(HBM, a) for a in (queries, new, cache, down.T, up)],
        [block] * sets
        + [
            shape_of((sets,) + block.shape, BF16),
            pltpu.VMEM(cache.shape[:3] + (cache.shape[3] + tall, HEAD_DIM), BF16),
            shape_of((slot + RANK // per, depth), BF16),
        ],
        [
            pltpu.VMEM(queries.shape, BF16),
            pltpu.VMEM(new.shape, BF16),
            pltpu.VMEM(up.shape, BF16),
            pltpu.SemaphoreType.DMA((4 + 2 * own,)),
        ],
    )
    cross = swap(cross, "tensor", sets)
    blocks = blocks[:1] + [swap(blocks[k], "tensor", k) for k in range(1, sets)]
    blocks += [cross[0]] + [swap(cross[k], "tensor", k) for k in range(1, sets)]
    factors = {0: factors}
    bit = spread // 2
    while bit > 1:
        factors |= {k ^ bit: swap(v, "fsdp", bit) for k, v in list(factors.items())}
        bit //= 2
    near_factors, blocks[1] = lax.optimization_barrier((factors[0], blocks[1]))

    half, quarter = spread // 2, spread // 4
    early = half + quarter
    fetched = quarter
    attended = call(
        functools.partial(attend_kernel, parts=parts, own=own, steps=steps),
        "attend",
        [(HBM, lengths)] + [(VMEM, b) for b in blocks] + [(HBM, weight), (VMEM, cache)],
        [shape_of((tall, width), BF16)] * parts
        + [pltpu.VMEM((early, depth, wide), BF16), pltpu.VMEM(cache.shape, BF16)],
        [
            pltpu.SMEM(lengths.shape, jnp.int32),
            pltpu.VMEM((parts, own * heads * steps, HEAD_DIM), BF16),
            pltpu.VMEM((parts, heads, tall, HEAD_DIM), F32),
            pltpu.VMEM((own, GROUP * steps, cache.shape[3]), F32),
            pltpu.VMEM((own, 2 * GROUP * steps, cache.shape[3]), BF16),
            pltpu.VMEM((own, GROUP * steps, cache.shape[3]), F32),
            pltpu.SemaphoreType.DMA(()),
            pltpu.SemaphoreType.DMA((early,)),
        ],
        alias={parts + 2: parts + 1},
    )
    attended, buffers = attended[:parts], [(0, attended[parts])]
    buffers += [
        (
            early,
            call(
                functools.partial(fetch_kernel, first=early),
                "fetch",
                [(ANY, attended[0]), (HBM, weight)],
                [pltpu.VMEM((fetched, depth, wide), BF16)],
                [pltpu.SemaphoreType.DMA((fetched,))],
                cost=pl.CostEstimate(
                    flops=0, bytes_accessed=2 * fetched * depth * wide, transcendentals=0
                ),
            )[0],
        )
    ]
    factors[1] = swap(near_factors, "fsdp", 1)
    attended, factors = lax.optimization_barrier((list(attended), factors))
    factors |= {k ^ 1: swap(v, "fsdp", 1) for k, v in list(factors.items()) if k > 1}
    got = {k: swap(attended[k], "tensor", k) for k in range(parts - 1, 0, -1)}
    attended = [attended[0]] + [got[k] for k in range(1, parts)]

    order = sorted(range(parts), key=lambda k: format(k, "08b")[::-1])
    attended = [attended[k] for k in order]

    def reduce(keep, send):
        bit = 1
        while True:
            got = swap(send, "tensor", bit)
            bit *= 2
            if bit == sets:
                return keep, got
            both = keep + got.astype(F32)
            half = both.shape[0] // 2
            keep, send = both[:half], both[half:].astype(BF16)

    def reduce_low(keep, send):
        bit = 1
        while True:
            both = fold_low(keep, swap(send, "tensor", bit))
            bit *= 2
            if bit == sets:
                return both
            half = both.shape[0] // 2
            keep, send = both[:half], jnp.concatenate(split(both[half:]), axis=1)

    keep, send, buffers = project(attended, weight, buffers, 0, spread, half)
    far_keep, far_got = reduce(keep, send)

    down_rows, ups = call(
        functools.partial(collect_kernel, slot=slot),
        "collect",
        [(ANY, keep)] + [(VMEM, factors[k]) for k in range(spread)],
        [shape_of((RANK, depth), BF16), shape_of((spread, RANK, cut), BF16)],
    )
    low_keep, low_send = call(
        lower_kernel,
        "lower",
        [(VMEM, a) for a in (*attended, down_rows)],
        [shape_of((sets * tall, RANK), F32), shape_of((sets * tall, 2 * RANK), BF16)],
    )
    low = reduce_low(low_keep, low_send)
    ordered = cut % HEAD_DIM != 0
    if ordered:
        ups = lax.all_gather(up, ("fsdp", "tensor"), axis=1, tiled=True)
        ups = ups.reshape(RANK, spread, 2, wide)
        top = lax.axis_index("tensor") // sets
        ups = lax.dynamic_index_in_dim(ups, top, 2, keepdims=False)
        up_sets = {0: ups.reshape(RANK, half_width)}
    else:
        up_sets = {0: ups}
        bit = sets // 2
        while bit:
            up_sets |= {k ^ bit: swap(u, "tensor", bit) for k, u in list(up_sets.items())}
            bit //= 2

    far = far_keep + far_got.astype(F32)
    low_parts = jnp.concatenate(split(low), axis=1)
    message = jnp.concatenate([far[tall:].astype(BF16), low_parts[tall:], low_parts[:tall]], axis=1)
    near = []

    def add_near(low, high, ahead):
        nonlocal buffers
        keep, send, buffers = project(attended, weight, buffers, low, high, ahead)
        near.append(reduce(keep, send))

    a, b = spread + quarter, 2 * spread - quarter
    add_near(spread, a, quarter)
    message, attended = lax.optimization_barrier((message, attended))
    message = swap(message, "tensor", sets)
    add_near(a, b, quarter)
    add_near(b, 2 * spread, 0)
    near_got, low_got = message[:, :half_width], message[:, half_width:]

    ups = [up_sets[k] for k in range(len(up_sets))]
    near_keep, near_send = call(
        functools.partial(adapt_kernel, pieces=len(near), sets=len(ups), ordered=ordered),
        "adapt",
        [(VMEM, a) for a in (low, low_got, *[k for k, _ in near], *[g for _, g in near], *ups)],
        [shape_of((tall, half_width), F32), shape_of((tall, half_width), BF16)],
        [pltpu.VMEM((2 * tall, half_width), F32)],
    )
    far_got = swap(near_send, "tensor", sets)

    return call(
        functools.partial(finish_kernel, own=own, steps=steps, strips=spread),
        "finish",
        [(VMEM, a) for a in (far[:tall], far_got, near_keep, near_got)],
        [shape_of((steps, own, weight.shape[1]), BF16)],
    )[0]


def solution(mesh):
    return jax.shard_map(
        shards,
        mesh=mesh,
        in_specs=(
            P(None, ("groups", "fsdp"), "tensor"),
            P(("groups", "fsdp", "tensor"), None, None, None, None),
            P(None, ("groups", "fsdp"), "tensor"),
            P(("groups", "fsdp", "tensor")),
            P("tensor", None),
            P("tensor", "fsdp"),
            P(None, ("fsdp", "tensor")),
        ),
        out_specs=P(None, ("groups", "fsdp", "tensor"), None),
        check_vma=False,
    )
```

```python
import functools

import jax
import jax.numpy as jnp
from jax import lax
from jax.experimental import pallas as pl
from jax.experimental.pallas import tpu as pltpu
from jax.sharding import PartitionSpec as P

HEADS = 64
KV_HEADS = 8
HEAD_DIM = 128
GROUP = HEADS // KV_HEADS
RANK = 64
LOG2_E = 1.4426950408889634
SCALE = 2.0
BF16 = jnp.bfloat16
F32 = jnp.float32
VMEM = pl.BlockSpec(memory_space=pltpu.VMEM)
ANY = pl.BlockSpec(memory_space=pl.ANY)
HBM = pl.BlockSpec(memory_space=pltpu.HBM)
ROW_ROW = (((1,), (1,)), ((), ()))
shape_of = jax.ShapeDtypeStruct


def dot(a, b):
    return jnp.dot(a, b, preferred_element_type=F32)


def dot_rows(a, b):
    return lax.dot_general(a, b, ROW_ROW, preferred_element_type=F32)


def call(kernel, name, ins, outs, scratch=(), mib=6, cost=None, alias=None):
    specs, args = zip(*ins)
    args = [
        pltpu.with_memory_space_constraint(a, pltpu.HBM) if s is HBM else a for s, a in ins
    ]
    return pl.pallas_call(
        kernel,
        in_specs=list(specs),
        out_specs=[VMEM] * len(outs),
        out_shape=list(outs),
        scratch_shapes=list(scratch),
        input_output_aliases=alias or {},
        compiler_params=pltpu.CompilerParams(vmem_limit_bytes=mib * 2**20),
        cost_estimate=cost,
        name=name,
    )(*args)


def split(x):
    high = x.astype(BF16)
    return high, (x - high.astype(F32)).astype(BF16)


def log2(n):
    return n.bit_length() - 1


def strip_copies(weight_hbm, strips_ref, sem, first):
    count, _, wide = strips_ref.shape
    spread = weight_hbm.shape[1] // (2 * wide)
    top = lax.axis_index("tensor") >> (log2(lax.axis_size("tensor")) - 1)
    copies = []
    for i in range(count):
        half = top if first + i >= spread else 1 - top
        start = pl.multiple_of((2 * ((first + i) % spread) + half) * wide, wide)
        copies.append(
            pltpu.make_async_copy(
                weight_hbm.at[:, pl.ds(start, wide)], strips_ref.at[i], sem.at[i]
            )
        )
    return copies


def stage_kernel(after_ref, cache_hbm, cache_ref, sem, *, own):
    slots = pl.ds(0, cache_hbm.shape[3])
    copies = [
        pltpu.make_async_copy(
            cache_hbm.at[r, part], cache_ref.at[r, part, :, slots], sem.at[r, part]
        )
        for r in range(own)
        for part in range(2)
    ]
    for copy in copies:
        copy.start()
    for copy in copies:
        copy.wait()


def pack_kernel(query_hbm, new_hbm, down_hbm, up_hbm, *refs, parts, own, steps):
    *block_refs, factor_ref, query_ref, new_ref, up_ref, sem = refs
    slot, depth = down_hbm.shape
    pairs = [
        (query_hbm, query_ref),
        (new_hbm, new_ref),
        (up_hbm, up_ref),
        (down_hbm, factor_ref.at[pl.ds(0, slot)]),
    ]
    copies = [pltpu.make_async_copy(*pair, sem.at[i]) for i, pair in enumerate(pairs)]
    for copy in copies:
        copy.start()
    me = lax.axis_index("tensor")
    count = steps * parts * own
    i = lax.broadcasted_iota(jnp.int32, (count, count), 0)
    j = lax.broadcasted_iota(jnp.int32, (count, count), 1)
    step_out = i & (steps - 1)
    row_out = (i >> log2(steps)) & (own - 1)
    part_out = (i >> log2(steps * own)) ^ me
    source = step_out * (parts * own) + part_out * own + row_out
    select = jnp.where(source == j, 1.0, 0.0).astype(BF16)
    for copy in copies[:3]:
        copy.wait()
    queries = dot(select, query_ref[...].reshape(count, query_ref.shape[2]))
    new = dot(select, new_ref[...].reshape(count, new_ref.shape[2]))
    heads = queries.shape[1] // HEAD_DIM
    pieces = new.shape[1] // HEAD_DIM
    tall = own * steps
    for k in range(parts):
        q = queries[k * tall : (k + 1) * tall]
        n = new[k * tall : (k + 1) * tall]
        tiles = [
            q[r * steps : (r + 1) * steps, h * HEAD_DIM : (h + 1) * HEAD_DIM]
            for r in range(own)
            for h in range(heads)
        ]
        tiles += [n[:, c * HEAD_DIM : (c + 1) * HEAD_DIM] for c in range(pieces)]
        block = jnp.concatenate(tiles, axis=0).astype(BF16)
        if k < parts // 2:
            block_refs[k][...] = block
        else:
            block_refs[-1][k - parts // 2] = block
    cut = up_ref.shape[1]
    per = depth // cut
    tall = RANK // per
    for c in range(per):
        factor_ref[slot : slot + tall, c * cut : (c + 1) * cut] = up_ref[c * tall : (c + 1) * tall, :]
    for copy in copies[3:]:
        copy.wait()


def attend_kernel(length_hbm, *refs, parts, own, steps):
    block_refs, refs = refs[:parts], refs[parts:]
    weight_hbm, refs = refs[0], refs[2:]
    out_refs, refs = refs[:parts], refs[parts:]
    strips_ref, cache_ref, length_ref, held_ref, attended_ref = refs[:5]
    scores_ref, weights_ref, mask_ref, length_sem, sem = refs[5:]
    length_copy = pltpu.make_async_copy(length_hbm, length_ref, length_sem)
    length_copy.start()
    heads = HEADS // parts
    pieces = 2 * KV_HEADS // parts
    query_rows = own * heads * steps
    tall = own * steps
    slots = cache_ref.shape[3] - tall
    count = GROUP * steps
    weight_copies = strip_copies(weight_hbm, strips_ref, sem, 0)
    for copy in weight_copies:
        copy.start()

    me = lax.axis_index("tensor")
    for k, block_ref in enumerate(block_refs):
        held_ref[me ^ k] = block_ref[0:query_rows, :]
        for c in range(pieces):
            piece = (me ^ k) * pieces + c
            start = query_rows + c * tall
            for r in range(own):
                cache_ref[r, piece >> log2(KV_HEADS), piece & (KV_HEADS - 1), slots : slots + tall, :] = (
                    block_ref[start : start + tall, :]
                )

    def queries(r, g):
        if heads >= GROUP:
            groups = heads // GROUP
            start = (r * heads + (g & (groups - 1)) * GROUP) * steps
            return held_ref[g >> log2(groups), pl.ds(pl.multiple_of(start, count), count), :]
        span = GROUP // heads
        start = pl.multiple_of(r * heads * steps, heads * steps)
        found = [held_ref[g * span + i, pl.ds(start, heads * steps), :] for i in range(span)]
        return jnp.concatenate(found, axis=0)

    slot = lax.broadcasted_iota(jnp.int32, (count, slots + tall), 1)
    step = lax.broadcasted_iota(jnp.int32, (count, slots + tall), 0) & (steps - 1)
    length_copy.wait()
    for r in range(own):
        fresh = slot - slots - r * steps
        valid = (slot < length_ref[r]) | ((fresh >= 0) & (fresh <= step))
        mask_ref[r] = jnp.where(valid, 0.0, -1e30)
    ones = jnp.ones((slots + tall, HEAD_DIM), BF16)

    def turn(i, _):
        scored = jnp.minimum(i, KV_HEADS - 1)
        summed = jnp.maximum(i - 2, 0)
        rows = range(own)
        mixed = [
            dot(weights_ref[r], jnp.concatenate([cache_ref[r, 1, summed], ones], axis=1)) for r in rows
        ]
        before = [scores_ref[r] for r in rows]
        weights = [jnp.exp2(b - b.max(-1, keepdims=True)) for b in before]
        scores = [
            dot_rows(queries(r, scored), cache_ref[r, 0, scored]) * (HEAD_DIM**-0.5 * LOG2_E)
            + mask_ref[r]
            for r in rows
        ]
        for r in rows:
            weights_ref[r] = jnp.concatenate(split(weights[r]), axis=0)
            scores_ref[r] = scores[r]
            total = mixed[r][:count] + mixed[r][count:]
            total = total[:, :HEAD_DIM] / total[:, HEAD_DIM:]
            for h in range(GROUP):
                head = summed * GROUP + h
                attended_ref[
                    head >> log2(heads), head & (heads - 1), r * steps : (r + 1) * steps, :
                ] = total[h * steps : (h + 1) * steps]
        return 0

    lax.fori_loop(0, KV_HEADS + 2, turn, 0, unroll=2)
    for k in range(parts):
        for h in range(heads):
            out_refs[k][:, h * HEAD_DIM : (h + 1) * HEAD_DIM] = attended_ref[me ^ k, h].astype(BF16)
    for copy in weight_copies:
        copy.wait()


def collect_kernel(*refs, slot):
    _, *factor_refs, down_ref, up_ref = refs
    me = lax.axis_index("fsdp")
    cut = up_ref.shape[2]
    per = down_ref.shape[1] // cut
    tall = RANK // per
    for k, factor_ref in enumerate(factor_refs):
        down_ref[pl.ds(pl.multiple_of((me ^ k) * slot, slot), slot), :] = factor_ref[0:slot, :]
        for c in range(per):
            up_ref[k, c * tall : (c + 1) * tall, :] = factor_ref[
                slot : slot + tall, c * cut : (c + 1) * cut
            ]


def fetch_kernel(after_ref, weight_hbm, strips_ref, sem, *, first):
    copies = strip_copies(weight_hbm, strips_ref, sem, first)
    for copy in copies:
        copy.start()
    for copy in copies:
        copy.wait()


def project_kernel(*refs, parts, spans, ahead, first):
    attended_refs, refs = refs[:parts], refs[parts:]
    held_refs, refs = refs[: len(spans)], refs[len(spans) :]
    weight_hbm, keep_ref, send_ref, refs = refs[0], refs[1], refs[2], refs[3:]
    copies = []
    if ahead:
        ahead_ref, rows_ref, sem = refs
        copies = strip_copies(weight_hbm, ahead_ref, sem, first)
    else:
        rows_ref = refs[0]
    for copy in copies:
        copy.start()
    tall = attended_refs[0].shape[0]
    for k, attended_ref in enumerate(attended_refs):
        rows_ref[k * tall : (k + 1) * tall, :] = attended_ref[...]
    half = rows_ref.shape[0] // 2
    place = 0
    for strips_ref, (low, high) in zip(held_refs, spans):
        wide = strips_ref.shape[2]

        @pl.loop(low, high + jnp.minimum(lax.axis_index("tensor"), 0))
        def _(i, strips_ref=strips_ref, place=place - low):
            out = dot(rows_ref[...], strips_ref[i])
            lanes = pl.ds(pl.multiple_of((place + i) * wide, wide), wide)
            keep_ref[:, lanes] = out[:half]
            send_ref[:, lanes] = out[half:].astype(BF16)

        place += high - low
    for copy in copies:
        copy.wait()


def project(attended, weight, buffers, low, high, ahead=0):
    parts = len(attended)
    tall, depth = attended[0].shape
    half = parts * tall // 2
    held, spans = [], []
    for first, buffer in buffers:
        a, b = max(low - first, 0), min(high - first, buffer.shape[0])
        if a < b:
            held.append(buffer)
            spans.append((a, b))
    wide = held[0].shape[2]
    width = wide * (high - low)
    next_strip = buffers[-1][0] + buffers[-1][1].shape[0]
    outs = [shape_of((half, width), F32), shape_of((half, width), BF16)]
    ins = [(VMEM, a) for a in attended] + [(VMEM, h) for h in held] + [(HBM, weight)]
    scratch = [pltpu.VMEM((parts * tall, depth), BF16)]
    if ahead:
        outs += [pltpu.VMEM((ahead, depth, wide), BF16)]
        scratch += [pltpu.SemaphoreType.DMA((ahead,))]
    kernel = functools.partial(
        project_kernel, parts=parts, spans=spans, ahead=ahead, first=next_strip
    )
    cost = pl.CostEstimate(
        flops=2 * parts * tall * depth * width, bytes_accessed=2 * depth * width, transcendentals=0
    )
    keep, send, *rest = call(kernel, "project", ins, outs, scratch, cost=cost)
    return keep, send, buffers + [(next_strip, rest[0])] if ahead else buffers


def lower_kernel(*refs):
    *attended_refs, down_ref, keep_ref, send_ref = refs
    half = len(attended_refs) // 2
    for first, last in ((0, half), (half, 2 * half)):
        rows = jnp.concatenate([a[...] for a in attended_refs[first:last]], axis=0)
        low = dot_rows(rows, down_ref[...])
        if first:
            send_ref[...] = jnp.concatenate(split(low), axis=1)
        else:
            keep_ref[...] = low


def handoff_kernel(send_ref, *refs, parts, slot):
    attended_refs, refs = refs[:parts], refs[parts:]
    *factor_refs, keep_ref, up_ref, handoff_ref, down_ref = refs
    collect_kernel(None, *factor_refs, down_ref, up_ref, slot=slot)
    half, width = send_ref.shape
    handoff_ref[:, :width] = send_ref[...]
    cut = up_ref.shape[2]
    for k in range(up_ref.shape[0]):
        for j in range(RANK // half):
            handoff_ref[:, width : width + cut] = up_ref[k, j * half : (j + 1) * half, :]
            width += cut
    rows = [
        jnp.concatenate([a[...] for a in attended_refs[i : i + parts // 2]], axis=0)
        for i in (0, parts // 2)
    ]
    keep_ref[...] = dot_rows(rows[0], down_ref[...])
    handoff_ref[:, width:] = jnp.concatenate(split(dot_rows(rows[1], down_ref[...])), axis=1)


def fold_low(keep, got):
    return keep + got[:, :RANK].astype(F32) + got[:, RANK:].astype(F32)


def adapt_kernel(*refs, pieces, sets, ordered):
    low_ref, low_got_ref, refs = refs[0], refs[1], refs[2:]
    keep_refs, refs = refs[:pieces], refs[pieces:]
    got_refs, refs = refs[:pieces], refs[pieces:]
    *up_refs, own_ref, send_ref, extra_ref = refs
    me, place = lax.axis_index("tensor"), lax.axis_index("fsdp")
    half = low_ref.shape[0] // 2
    got = low_got_ref[...]
    got = jnp.concatenate([got[:, : 2 * RANK], got[:, 2 * RANK :]], axis=0)
    low = SCALE * fold_low(low_ref[...], got)
    low = jnp.concatenate(split(low), axis=0)
    if ordered:
        both = dot(low, up_refs[0][...])
        extra_ref[...] = both[: 2 * half] + both[2 * half :]
    else:
        spread, _, cut = up_refs[0].shape
        for kt in range(sets):
            for kf in range(spread):
                if kt < len(up_refs) and len(up_refs[kt].shape) == 3:
                    factor = up_refs[kt][kf]
                else:
                    tall = up_refs[kt].shape[0]
                    first = extra_ref.shape[1] + kf * (RANK // tall) * cut
                    factor = jnp.concatenate(
                        [
                            up_refs[kt][:, first + j * cut : first + (j + 1) * cut]
                            for j in range(RANK // tall)
                        ],
                        axis=0,
                    )
                both = dot(low, factor)
                column = (place ^ kf) * sets + ((me ^ kt) & (sets - 1))
                start = pl.multiple_of(column * cut, cut)
                extra_ref[:, pl.ds(start, cut)] = both[: 2 * half] + both[2 * half :]
    first = 0
    for keep_ref, got_ref in zip(keep_refs, got_refs):
        lanes = slice(first, first + keep_ref.shape[1])
        first += keep_ref.shape[1]
        total = keep_ref[...] + got_ref[...].astype(F32) + extra_ref[:, lanes]
        own_ref[:, lanes] = total[:half]
        send_ref[:, lanes] = total[half:].astype(BF16)


def finish_kernel(far_ref, far_got_ref, near_ref, near_got_ref, out_ref, *, own, steps, strips):
    top = lax.axis_index("tensor") >> (log2(lax.axis_size("tensor")) - 1)
    wide = near_ref.shape[1] // strips
    for keep_ref, got_ref, half in ((near_ref, near_got_ref, top), (far_ref, far_got_ref, 1 - top)):
        for i in range(strips):
            lanes = slice(i * wide, (i + 1) * wide)
            total = (keep_ref[:, lanes] + got_ref[:, lanes].astype(F32)).astype(BF16)
            start = pl.multiple_of((2 * i + half) * wide, wide)
            for r in range(own):
                out_ref[:, r, pl.ds(start, wide)] = total[r * steps : (r + 1) * steps]


def shards(queries, cache, new, lengths, weight, down, up):
    parts, spread = lax.axis_size("tensor"), lax.axis_size("fsdp")
    steps, rows, width = queries.shape
    own = rows // parts
    tall = own * steps
    depth, slot = down.shape
    cut = up.shape[1]
    heads, pieces = width // HEAD_DIM, new.shape[2] // HEAD_DIM
    sets = parts // 2
    wide = sets * cut
    half_width = spread * wide
    swap = lambda x, axis, k: lax.ppermute(
        x, axis, [(i, i ^ k) for i in range(lax.axis_size(axis))]
    )

    block = shape_of((own * heads * steps + pieces * tall, HEAD_DIM), BF16)
    per = depth // cut
    *blocks, cross, factors = call(
        functools.partial(pack_kernel, parts=parts, own=own, steps=steps),
        "pack",
        [(HBM, a) for a in (queries, new, down.T, up)],
        [block] * sets
        + [shape_of((sets,) + block.shape, BF16), shape_of((slot + RANK // per, depth), BF16)],
        [
            pltpu.VMEM(queries.shape, BF16),
            pltpu.VMEM(new.shape, BF16),
            pltpu.VMEM(up.shape, BF16),
            pltpu.SemaphoreType.DMA((4,)),
        ],
    )
    (cache,) = call(
        functools.partial(stage_kernel, own=own),
        "stage",
        [(ANY, blocks[0]), (HBM, cache)],
        [pltpu.VMEM(cache.shape[:3] + (cache.shape[3] + tall, HEAD_DIM), BF16)],
        [pltpu.SemaphoreType.DMA((own, 2))],
        cost=pl.CostEstimate(flops=0, bytes_accessed=2 * cache.size, transcendentals=0),
    )
    cross = swap(cross, "tensor", sets)
    blocks = blocks[:1] + [swap(blocks[k], "tensor", k) for k in range(1, sets)]
    blocks += [cross[0]] + [swap(cross[k], "tensor", k) for k in range(1, sets)]
    factors = {0: factors}
    bit = spread // 2
    while bit > 1:
        factors |= {k ^ bit: swap(v, "fsdp", bit) for k, v in list(factors.items())}
        bit //= 2
    near_factors, blocks[1] = lax.optimization_barrier((factors[0], blocks[1]))

    half, quarter = spread // 2, spread // 4
    early = half + quarter
    fetched = quarter
    attended = call(
        functools.partial(attend_kernel, parts=parts, own=own, steps=steps),
        "attend",
        [(HBM, lengths)] + [(VMEM, b) for b in blocks] + [(HBM, weight), (VMEM, cache)],
        [shape_of((tall, width), BF16)] * parts
        + [pltpu.VMEM((early, depth, wide), BF16), pltpu.VMEM(cache.shape, BF16)],
        [
            pltpu.SMEM(lengths.shape, jnp.int32),
            pltpu.VMEM((parts, own * heads * steps, HEAD_DIM), BF16),
            pltpu.VMEM((parts, heads, tall, HEAD_DIM), F32),
            pltpu.VMEM((own, GROUP * steps, cache.shape[3]), F32),
            pltpu.VMEM((own, 2 * GROUP * steps, cache.shape[3]), BF16),
            pltpu.VMEM((own, GROUP * steps, cache.shape[3]), F32),
            pltpu.SemaphoreType.DMA(()),
            pltpu.SemaphoreType.DMA((early,)),
        ],
        alias={parts + 2: parts + 1},
    )
    attended, buffers = attended[:parts], [(0, attended[parts])]
    buffers += [
        (
            early,
            call(
                functools.partial(fetch_kernel, first=early),
                "fetch",
                [(ANY, attended[0]), (HBM, weight)],
                [pltpu.VMEM((fetched, depth, wide), BF16)],
                [pltpu.SemaphoreType.DMA((fetched,))],
                cost=pl.CostEstimate(
                    flops=0, bytes_accessed=2 * fetched * depth * wide, transcendentals=0
                ),
            )[0],
        )
    ]
    factors[1] = swap(near_factors, "fsdp", 1)
    attended, factors = lax.optimization_barrier((list(attended), factors))
    factors |= {k ^ 1: swap(v, "fsdp", 1) for k, v in list(factors.items()) if k > 1}
    got = {k: swap(attended[k], "tensor", k) for k in range(parts - 1, 0, -1)}
    attended = [attended[0]] + [got[k] for k in range(1, parts)]

    order = sorted(range(parts), key=lambda k: format(k, "08b")[::-1])
    attended = [attended[k] for k in order]

    def reduce(keep, send):
        bit = 1
        while True:
            got = swap(send, "tensor", bit)
            bit *= 2
            if bit == sets:
                return keep, got
            both = keep + got.astype(F32)
            half = both.shape[0] // 2
            keep, send = both[:half], both[half:].astype(BF16)

    def reduce_low(keep, send):
        bit = 1
        while True:
            both = fold_low(keep, swap(send, "tensor", bit))
            bit *= 2
            if bit == sets:
                return both
            half = both.shape[0] // 2
            keep, send = both[:half], jnp.concatenate(split(both[half:]), axis=1)

    keep, send, buffers = project(attended, weight, buffers, 0, spread, half)
    ordered = cut % HEAD_DIM != 0
    if sets == 2 and not ordered:
        inner = (spread * RANK * cut) // (2 * tall)
        low_keep, ups, handoff = call(
            functools.partial(handoff_kernel, parts=parts, slot=slot),
            "handoff",
            [(VMEM, a) for a in (send, *attended, *[factors[k] for k in range(spread)])],
            [
                shape_of((2 * tall, RANK), F32),
                shape_of((spread, RANK, cut), BF16),
                shape_of((2 * tall, half_width + inner + 2 * RANK), BF16),
            ],
            [pltpu.VMEM((RANK, depth), BF16)],
        )
        handoff = swap(handoff, "tensor", 1)
        far_keep, far_got = keep, handoff[:, :half_width]
        low = fold_low(low_keep, handoff[:, half_width + inner :])
        up_sets = {0: ups, 1: handoff}
    else:
        far_keep, far_got = reduce(keep, send)

        down_rows, ups = call(
            functools.partial(collect_kernel, slot=slot),
            "collect",
            [(ANY, keep)] + [(VMEM, factors[k]) for k in range(spread)],
            [shape_of((RANK, depth), BF16), shape_of((spread, RANK, cut), BF16)],
        )
        low_keep, low_send = call(
            lower_kernel,
            "lower",
            [(VMEM, a) for a in (*attended, down_rows)],
            [shape_of((sets * tall, RANK), F32), shape_of((sets * tall, 2 * RANK), BF16)],
        )
        low = reduce_low(low_keep, low_send)
        if ordered:
            ups = lax.all_gather(up, ("fsdp", "tensor"), axis=1, tiled=True)
            ups = ups.reshape(RANK, spread, 2, wide)
            top = lax.axis_index("tensor") // sets
            ups = lax.dynamic_index_in_dim(ups, top, 2, keepdims=False)
            up_sets = {0: ups.reshape(RANK, half_width)}
        else:
            up_sets = {0: ups}
            bit = sets // 2
            while bit:
                up_sets |= {k ^ bit: swap(u, "tensor", bit) for k, u in list(up_sets.items())}
                bit //= 2

    far = far_keep + far_got.astype(F32)
    low_parts = jnp.concatenate(split(low), axis=1)
    message = jnp.concatenate([far[tall:].astype(BF16), low_parts[tall:], low_parts[:tall]], axis=1)
    near = []

    def add_near(low, high, ahead):
        nonlocal buffers
        keep, send, buffers = project(attended, weight, buffers, low, high, ahead)
        near.append(reduce(keep, send))

    a, b = spread + quarter, 2 * spread - quarter
    add_near(spread, a, quarter)
    message, attended = lax.optimization_barrier((message, attended))
    message = swap(message, "tensor", sets)
    add_near(a, b, quarter)
    add_near(b, 2 * spread, 0)
    near_got, low_got = message[:, :half_width], message[:, half_width:]

    ups = [up_sets[k] for k in range(len(up_sets))]
    near_keep, near_send = call(
        functools.partial(adapt_kernel, pieces=len(near), sets=sets, ordered=ordered),
        "adapt",
        [(VMEM, a) for a in (low, low_got, *[k for k, _ in near], *[g for _, g in near], *ups)],
        [shape_of((tall, half_width), F32), shape_of((tall, half_width), BF16)],
        [pltpu.VMEM((2 * tall, half_width), F32)],
    )
    far_got = swap(near_send, "tensor", sets)

    return call(
        functools.partial(finish_kernel, own=own, steps=steps, strips=spread),
        "finish",
        [(VMEM, a) for a in (far[:tall], far_got, near_keep, near_got)],
        [shape_of((steps, own, weight.shape[1]), BF16)],
    )[0]


def solution(mesh):
    return jax.shard_map(
        shards,
        mesh=mesh,
        in_specs=(
            P(None, ("groups", "fsdp"), "tensor"),
            P(("groups", "fsdp", "tensor"), None, None, None, None),
            P(None, ("groups", "fsdp"), "tensor"),
            P(("groups", "fsdp", "tensor")),
            P("tensor", None),
            P("tensor", "fsdp"),
            P(None, ("fsdp", "tensor")),
        ),
        out_specs=P(None, ("groups", "fsdp", "tensor"), None),
        check_vma=False,
    )
```

```python
import functools

import jax
import jax.numpy as jnp
from jax import lax
from jax.experimental import pallas as pl
from jax.experimental.pallas import tpu as pltpu
from jax.sharding import PartitionSpec as P

HEADS = 64
KV_HEADS = 8
HEAD_DIM = 128
GROUP = HEADS // KV_HEADS
RANK = 64
LOG2_E = 1.4426950408889634
SCALE = 2.0
BF16 = jnp.bfloat16
F32 = jnp.float32
VMEM = pl.BlockSpec(memory_space=pltpu.VMEM)
ANY = pl.BlockSpec(memory_space=pl.ANY)
HBM = pl.BlockSpec(memory_space=pltpu.HBM)
ROW_ROW = (((1,), (1,)), ((), ()))
shape_of = jax.ShapeDtypeStruct


def dot(a, b):
    return jnp.dot(a, b, preferred_element_type=F32)


def dot_rows(a, b):
    return lax.dot_general(a, b, ROW_ROW, preferred_element_type=F32)


def call(kernel, name, ins, outs, scratch=(), mib=6, cost=None, alias=None):
    specs, args = zip(*ins)
    args = [
        pltpu.with_memory_space_constraint(a, pltpu.HBM) if s is HBM else a for s, a in ins
    ]
    return pl.pallas_call(
        kernel,
        in_specs=list(specs),
        out_specs=[VMEM] * len(outs),
        out_shape=list(outs),
        scratch_shapes=list(scratch),
        input_output_aliases=alias or {},
        compiler_params=pltpu.CompilerParams(vmem_limit_bytes=mib * 2**20),
        cost_estimate=cost,
        name=name,
    )(*args)


def split(x):
    high = x.astype(BF16)
    return high, (x - high.astype(F32)).astype(BF16)


def log2(n):
    return n.bit_length() - 1


def strip_copies(weight_hbm, strips_ref, sem, first):
    count, _, wide = strips_ref.shape
    spread = weight_hbm.shape[1] // (2 * wide)
    top = lax.axis_index("tensor") >> (log2(lax.axis_size("tensor")) - 1)
    copies = []
    for i in range(count):
        half = top if first + i >= spread else 1 - top
        start = pl.multiple_of((2 * ((first + i) % spread) + half) * wide, wide)
        copies.append(
            pltpu.make_async_copy(
                weight_hbm.at[:, pl.ds(start, wide)], strips_ref.at[i], sem.at[i]
            )
        )
    return copies


def stage_kernel(after_ref, cache_hbm, cache_ref, sem, *, own):
    slots = pl.ds(0, cache_hbm.shape[3])
    copies = [
        pltpu.make_async_copy(
            cache_hbm.at[r, part], cache_ref.at[r, part, :, slots], sem.at[r, part]
        )
        for r in range(own)
        for part in range(2)
    ]
    for copy in copies:
        copy.start()
    for copy in copies:
        copy.wait()


def pack_kernel(query_hbm, new_hbm, down_hbm, up_hbm, *refs, parts, own, steps):
    *block_refs, factor_ref, query_ref, new_ref, up_ref, sem = refs
    slot, depth = down_hbm.shape
    pairs = [
        (query_hbm, query_ref),
        (new_hbm, new_ref),
        (up_hbm, up_ref),
        (down_hbm, factor_ref.at[pl.ds(0, slot)]),
    ]
    copies = [pltpu.make_async_copy(*pair, sem.at[i]) for i, pair in enumerate(pairs)]
    for copy in copies:
        copy.start()
    me = lax.axis_index("tensor")
    count = steps * parts * own
    i = lax.broadcasted_iota(jnp.int32, (count, count), 0)
    j = lax.broadcasted_iota(jnp.int32, (count, count), 1)
    step_out = i & (steps - 1)
    row_out = (i >> log2(steps)) & (own - 1)
    part_out = (i >> log2(steps * own)) ^ me
    source = step_out * (parts * own) + part_out * own + row_out
    select = jnp.where(source == j, 1.0, 0.0).astype(BF16)
    for copy in copies[:3]:
        copy.wait()
    queries = dot(select, query_ref[...].reshape(count, query_ref.shape[2]))
    new = dot(select, new_ref[...].reshape(count, new_ref.shape[2]))
    heads = queries.shape[1] // HEAD_DIM
    pieces = new.shape[1] // HEAD_DIM
    tall = own * steps
    for k in range(parts):
        q = queries[k * tall : (k + 1) * tall]
        n = new[k * tall : (k + 1) * tall]
        tiles = [
            q[r * steps : (r + 1) * steps, h * HEAD_DIM : (h + 1) * HEAD_DIM]
            for r in range(own)
            for h in range(heads)
        ]
        tiles += [n[:, c * HEAD_DIM : (c + 1) * HEAD_DIM] for c in range(pieces)]
        block = jnp.concatenate(tiles, axis=0).astype(BF16)
        if k < parts // 2:
            block_refs[k][...] = block
        else:
            block_refs[-1][k - parts // 2] = block
    cut = up_ref.shape[1]
    per = depth // cut
    tall = RANK // per
    for c in range(per):
        factor_ref[slot : slot + tall, c * cut : (c + 1) * cut] = up_ref[c * tall : (c + 1) * tall, :]
    for copy in copies[3:]:
        copy.wait()


def attend_kernel(length_hbm, *refs, parts, own, steps):
    block_refs, refs = refs[:parts], refs[parts:]
    weight_hbm, refs = refs[0], refs[2:]
    out_refs, refs = refs[:parts], refs[parts:]
    strips_ref, cache_ref, length_ref, held_ref, attended_ref = refs[:5]
    scores_ref, weights_ref, mask_ref, length_sem, sem = refs[5:]
    length_copy = pltpu.make_async_copy(length_hbm, length_ref, length_sem)
    length_copy.start()
    heads = HEADS // parts
    pieces = 2 * KV_HEADS // parts
    query_rows = own * heads * steps
    tall = own * steps
    slots = cache_ref.shape[3] - tall
    count = GROUP * steps
    weight_copies = strip_copies(weight_hbm, strips_ref, sem, 0)
    for copy in weight_copies:
        copy.start()

    me = lax.axis_index("tensor")
    for k, block_ref in enumerate(block_refs):
        held_ref[me ^ k] = block_ref[0:query_rows, :]
        for c in range(pieces):
            piece = (me ^ k) * pieces + c
            start = query_rows + c * tall
            for r in range(own):
                cache_ref[r, piece >> log2(KV_HEADS), piece & (KV_HEADS - 1), slots : slots + tall, :] = (
                    block_ref[start : start + tall, :]
                )

    def queries(r, g):
        if heads >= GROUP:
            groups = heads // GROUP
            start = (r * heads + (g & (groups - 1)) * GROUP) * steps
            return held_ref[g >> log2(groups), pl.ds(pl.multiple_of(start, count), count), :]
        span = GROUP // heads
        start = pl.multiple_of(r * heads * steps, heads * steps)
        found = [held_ref[g * span + i, pl.ds(start, heads * steps), :] for i in range(span)]
        return jnp.concatenate(found, axis=0)

    slot = lax.broadcasted_iota(jnp.int32, (count, slots + tall), 1)
    step = lax.broadcasted_iota(jnp.int32, (count, slots + tall), 0) & (steps - 1)
    length_copy.wait()
    for r in range(own):
        fresh = slot - slots - r * steps
        valid = (slot < length_ref[r]) | ((fresh >= 0) & (fresh <= step))
        mask_ref[r] = jnp.where(valid, 0.0, -1e30)
    ones = jnp.ones((slots + tall, HEAD_DIM), BF16)

    def turn(i, _):
        scored = jnp.minimum(i, KV_HEADS - 1)
        summed = jnp.maximum(i - 2, 0)
        rows = range(own)
        mixed = [
            dot(weights_ref[r], jnp.concatenate([cache_ref[r, 1, summed], ones], axis=1)) for r in rows
        ]
        before = [scores_ref[r] for r in rows]
        weights = [jnp.exp2(b - b.max(-1, keepdims=True)) for b in before]
        scores = [
            dot_rows(queries(r, scored), cache_ref[r, 0, scored]) * (HEAD_DIM**-0.5 * LOG2_E)
            + mask_ref[r]
            for r in rows
        ]
        for r in rows:
            weights_ref[r] = jnp.concatenate(split(weights[r]), axis=0)
            scores_ref[r] = scores[r]
            total = mixed[r][:count] + mixed[r][count:]
            total = total[:, :HEAD_DIM] / total[:, HEAD_DIM:]
            for h in range(GROUP):
                head = summed * GROUP + h
                attended_ref[
                    head >> log2(heads), head & (heads - 1), pl.ds(r, steps, stride=own), :
                ] = total[h * steps : (h + 1) * steps]
        return 0

    lax.fori_loop(0, KV_HEADS + 2, turn, 0, unroll=2)
    for k in range(parts):
        for h in range(heads):
            out_refs[k][:, h * HEAD_DIM : (h + 1) * HEAD_DIM] = attended_ref[me ^ k, h].astype(BF16)
    for copy in weight_copies:
        copy.wait()


def collect_kernel(*refs, slot):
    _, *factor_refs, down_ref, up_ref = refs
    me = lax.axis_index("fsdp")
    cut = up_ref.shape[2]
    per = down_ref.shape[1] // cut
    tall = RANK // per
    for k, factor_ref in enumerate(factor_refs):
        down_ref[pl.ds(pl.multiple_of((me ^ k) * slot, slot), slot), :] = factor_ref[0:slot, :]
        for c in range(per):
            up_ref[k, c * tall : (c + 1) * tall, :] = factor_ref[
                slot : slot + tall, c * cut : (c + 1) * cut
            ]


def fetch_kernel(after_ref, weight_hbm, strips_ref, sem, *, first):
    copies = strip_copies(weight_hbm, strips_ref, sem, first)
    for copy in copies:
        copy.start()
    for copy in copies:
        copy.wait()


def project_kernel(*refs, parts, spans, ahead, first):
    attended_refs, refs = refs[:parts], refs[parts:]
    held_refs, refs = refs[: len(spans)], refs[len(spans) :]
    weight_hbm, keep_ref, send_ref, refs = refs[0], refs[1], refs[2], refs[3:]
    copies = []
    if ahead:
        ahead_ref, rows_ref, sem = refs
        copies = strip_copies(weight_hbm, ahead_ref, sem, first)
    else:
        rows_ref = refs[0]
    for copy in copies:
        copy.start()
    tall = attended_refs[0].shape[0]
    for k, attended_ref in enumerate(attended_refs):
        rows_ref[k * tall : (k + 1) * tall, :] = attended_ref[...]
    half = rows_ref.shape[0] // 2
    place = 0
    for strips_ref, (low, high) in zip(held_refs, spans):
        wide = strips_ref.shape[2]

        @pl.loop(low, high + jnp.minimum(lax.axis_index("tensor"), 0))
        def _(i, strips_ref=strips_ref, place=place - low):
            out = dot(rows_ref[...], strips_ref[i])
            lanes = pl.ds(pl.multiple_of((place + i) * wide, wide), wide)
            keep_ref[:, lanes] = out[:half]
            send_ref[:, lanes] = out[half:].astype(BF16)

        place += high - low
    for copy in copies:
        copy.wait()


def project(attended, weight, buffers, low, high, ahead=0):
    parts = len(attended)
    tall, depth = attended[0].shape
    half = parts * tall // 2
    held, spans = [], []
    for first, buffer in buffers:
        a, b = max(low - first, 0), min(high - first, buffer.shape[0])
        if a < b:
            held.append(buffer)
            spans.append((a, b))
    wide = held[0].shape[2]
    width = wide * (high - low)
    next_strip = buffers[-1][0] + buffers[-1][1].shape[0]
    outs = [shape_of((half, width), F32), shape_of((half, width), BF16)]
    ins = [(VMEM, a) for a in attended] + [(VMEM, h) for h in held] + [(HBM, weight)]
    scratch = [pltpu.VMEM((parts * tall, depth), BF16)]
    if ahead:
        outs += [pltpu.VMEM((ahead, depth, wide), BF16)]
        scratch += [pltpu.SemaphoreType.DMA((ahead,))]
    kernel = functools.partial(
        project_kernel, parts=parts, spans=spans, ahead=ahead, first=next_strip
    )
    cost = pl.CostEstimate(
        flops=2 * parts * tall * depth * width, bytes_accessed=2 * depth * width, transcendentals=0
    )
    keep, send, *rest = call(kernel, "project", ins, outs, scratch, cost=cost)
    return keep, send, buffers + [(next_strip, rest[0])] if ahead else buffers


def lower_kernel(*refs):
    *attended_refs, down_ref, keep_ref, send_ref = refs
    half = len(attended_refs) // 2
    for first, last in ((0, half), (half, 2 * half)):
        rows = jnp.concatenate([a[...] for a in attended_refs[first:last]], axis=0)
        low = dot_rows(rows, down_ref[...])
        if first:
            send_ref[...] = jnp.concatenate(split(low), axis=1)
        else:
            keep_ref[...] = low


def handoff_kernel(send_ref, *refs, parts, slot):
    attended_refs, refs = refs[:parts], refs[parts:]
    *factor_refs, keep_ref, up_ref, handoff_ref, down_ref = refs
    collect_kernel(None, *factor_refs, down_ref, up_ref, slot=slot)
    half, width = send_ref.shape
    handoff_ref[:, :width] = send_ref[...]
    cut = up_ref.shape[2]
    for k in range(up_ref.shape[0]):
        for j in range(RANK // half):
            handoff_ref[:, width : width + cut] = up_ref[k, j * half : (j + 1) * half, :]
            width += cut
    rows = [
        jnp.concatenate([a[...] for a in attended_refs[i : i + parts // 2]], axis=0)
        for i in (0, parts // 2)
    ]
    keep_ref[...] = dot_rows(rows[0], down_ref[...])
    handoff_ref[:, width:] = jnp.concatenate(split(dot_rows(rows[1], down_ref[...])), axis=1)


def fold_low(keep, got):
    return keep + got[:, :RANK].astype(F32) + got[:, RANK:].astype(F32)


def adapt_kernel(*refs, pieces, sets, ordered):
    low_ref, low_got_ref, refs = refs[0], refs[1], refs[2:]
    keep_refs, refs = refs[:pieces], refs[pieces:]
    got_refs, refs = refs[:pieces], refs[pieces:]
    *up_refs, own_ref, send_ref, extra_ref = refs
    me, place = lax.axis_index("tensor"), lax.axis_index("fsdp")
    half = low_ref.shape[0] // 2
    got = low_got_ref[...]
    got = jnp.concatenate([got[:, : 2 * RANK], got[:, 2 * RANK :]], axis=0)
    low = SCALE * fold_low(low_ref[...], got)
    low = jnp.concatenate(split(low), axis=0)
    if ordered:
        both = dot(low, up_refs[0][...])
        extra_ref[...] = both[: 2 * half] + both[2 * half :]
    else:
        spread, _, cut = up_refs[0].shape
        for kt in range(sets):
            for kf in range(spread):
                if kt < len(up_refs) and len(up_refs[kt].shape) == 3:
                    factor = up_refs[kt][kf]
                else:
                    tall = up_refs[kt].shape[0]
                    first = extra_ref.shape[1] + kf * (RANK // tall) * cut
                    factor = jnp.concatenate(
                        [
                            up_refs[kt][:, first + j * cut : first + (j + 1) * cut]
                            for j in range(RANK // tall)
                        ],
                        axis=0,
                    )
                both = dot(low, factor)
                column = (place ^ kf) * sets + ((me ^ kt) & (sets - 1))
                start = pl.multiple_of(column * cut, cut)
                extra_ref[:, pl.ds(start, cut)] = both[: 2 * half] + both[2 * half :]
    first = 0
    for keep_ref, got_ref in zip(keep_refs, got_refs):
        lanes = slice(first, first + keep_ref.shape[1])
        first += keep_ref.shape[1]
        total = keep_ref[...] + got_ref[...].astype(F32) + extra_ref[:, lanes]
        own_ref[:, lanes] = total[:half]
        send_ref[:, lanes] = total[half:].astype(BF16)


def join_kernel(keep_ref, low_keep_ref, handoff_ref, own_ref, message_ref, low_ref):
    half, width = own_ref.shape
    own_ref[...] = keep_ref[:half, :] + handoff_ref[:half, :width].astype(F32)
    total = keep_ref[half:, :] + handoff_ref[half:, :width].astype(F32)
    message_ref[:, :width] = total.astype(BF16)
    low = fold_low(low_keep_ref[...], handoff_ref[:, handoff_ref.shape[1] - 2 * RANK :])
    low_ref[...] = low
    parts = jnp.concatenate(split(low), axis=1)
    message_ref[:, width:] = jnp.concatenate([parts[half:], parts[:half]], axis=1)


def finish_kernel(far_ref, far_got_ref, near_ref, near_got_ref, out_ref, *, own, steps, strips):
    top = lax.axis_index("tensor") >> (log2(lax.axis_size("tensor")) - 1)
    wide = near_ref.shape[1] // strips
    for keep_ref, got_ref, half in ((near_ref, near_got_ref, top), (far_ref, far_got_ref, 1 - top)):
        for i in range(strips):
            lanes = slice(i * wide, (i + 1) * wide)
            total = (keep_ref[:, lanes] + got_ref[:, lanes].astype(F32)).astype(BF16)
            start = pl.multiple_of((2 * i + half) * wide, wide)
            out_ref[:, :, pl.ds(start, wide)] = total.reshape(steps, own, wide)


def shards(queries, cache, new, lengths, weight, down, up):
    parts, spread = lax.axis_size("tensor"), lax.axis_size("fsdp")
    steps, rows, width = queries.shape
    own = rows // parts
    tall = own * steps
    depth, slot = down.shape
    cut = up.shape[1]
    heads, pieces = width // HEAD_DIM, new.shape[2] // HEAD_DIM
    sets = parts // 2
    wide = sets * cut
    half_width = spread * wide
    swap = lambda x, axis, k: lax.ppermute(
        x, axis, [(i, i ^ k) for i in range(lax.axis_size(axis))]
    )

    block = shape_of((own * heads * steps + pieces * tall, HEAD_DIM), BF16)
    per = depth // cut
    *blocks, cross, factors = call(
        functools.partial(pack_kernel, parts=parts, own=own, steps=steps),
        "pack",
        [(HBM, a) for a in (queries, new, down.T, up)],
        [block] * sets
        + [shape_of((sets,) + block.shape, BF16), shape_of((slot + RANK // per, depth), BF16)],
        [
            pltpu.VMEM(queries.shape, BF16),
            pltpu.VMEM(new.shape, BF16),
            pltpu.VMEM(up.shape, BF16),
            pltpu.SemaphoreType.DMA((4,)),
        ],
    )
    (cache,) = call(
        functools.partial(stage_kernel, own=own),
        "stage",
        [(ANY, blocks[0]), (HBM, cache)],
        [pltpu.VMEM(cache.shape[:3] + (cache.shape[3] + tall, HEAD_DIM), BF16)],
        [pltpu.SemaphoreType.DMA((own, 2))],
        cost=pl.CostEstimate(flops=0, bytes_accessed=2 * cache.size, transcendentals=0),
    )
    cross = swap(cross, "tensor", sets)
    cross, cache = lax.optimization_barrier((cross, cache))
    blocks = blocks[:1] + [swap(blocks[k], "tensor", k) for k in range(1, sets)]
    blocks += [cross[0]] + [swap(cross[k], "tensor", k) for k in range(1, sets)]
    factors = {0: factors}
    bit = spread // 2
    while bit > 1:
        factors |= {k ^ bit: swap(v, "fsdp", bit) for k, v in list(factors.items())}
        bit //= 2

    half, quarter = spread // 2, spread // 4
    early = half + quarter
    fetched = quarter
    attended = call(
        functools.partial(attend_kernel, parts=parts, own=own, steps=steps),
        "attend",
        [(HBM, lengths)] + [(VMEM, b) for b in blocks] + [(HBM, weight), (VMEM, cache)],
        [shape_of((tall, width), BF16)] * parts
        + [pltpu.VMEM((early, depth, wide), BF16), pltpu.VMEM(cache.shape, BF16)],
        [
            pltpu.SMEM(lengths.shape, jnp.int32),
            pltpu.VMEM((parts, own * heads * steps, HEAD_DIM), BF16),
            pltpu.VMEM((parts, heads, tall, HEAD_DIM), F32),
            pltpu.VMEM((own, GROUP * steps, cache.shape[3]), F32),
            pltpu.VMEM((own, 2 * GROUP * steps, cache.shape[3]), BF16),
            pltpu.VMEM((own, GROUP * steps, cache.shape[3]), F32),
            pltpu.SemaphoreType.DMA(()),
            pltpu.SemaphoreType.DMA((early,)),
        ],
        alias={parts + 2: parts + 1},
    )
    attended, buffers = attended[:parts], [(0, attended[parts])]
    buffers += [
        (
            early,
            call(
                functools.partial(fetch_kernel, first=early),
                "fetch",
                [(ANY, attended[0]), (HBM, weight)],
                [pltpu.VMEM((fetched, depth, wide), BF16)],
                [pltpu.SemaphoreType.DMA((fetched,))],
                cost=pl.CostEstimate(
                    flops=0, bytes_accessed=2 * fetched * depth * wide, transcendentals=0
                ),
            )[0],
        )
    ]
    attended, factors = lax.optimization_barrier((list(attended), factors))
    factors |= {k ^ 1: swap(v, "fsdp", 1) for k, v in list(factors.items())}
    got = {k: swap(attended[k], "tensor", k) for k in range(parts - 1, 0, -1)}
    attended = [attended[0]] + [got[k] for k in range(1, parts)]

    order = sorted(range(parts), key=lambda k: format(k, "08b")[::-1])
    attended = [attended[k] for k in order]

    def reduce(keep, send):
        bit = 1
        while True:
            got = swap(send, "tensor", bit)
            bit *= 2
            if bit == sets:
                return keep, got
            both = keep + got.astype(F32)
            half = both.shape[0] // 2
            keep, send = both[:half], both[half:].astype(BF16)

    def reduce_low(keep, send):
        bit = 1
        while True:
            both = fold_low(keep, swap(send, "tensor", bit))
            bit *= 2
            if bit == sets:
                return both
            half = both.shape[0] // 2
            keep, send = both[:half], jnp.concatenate(split(both[half:]), axis=1)

    keep, send, buffers = project(attended, weight, buffers, 0, spread, half)
    ordered = cut % HEAD_DIM != 0
    if sets == 2 and not ordered:
        inner = (spread * RANK * cut) // (2 * tall)
        low_keep, ups, handoff = call(
            functools.partial(handoff_kernel, parts=parts, slot=slot),
            "handoff",
            [(VMEM, a) for a in (send, *attended, *[factors[k] for k in range(spread)])],
            [
                shape_of((2 * tall, RANK), F32),
                shape_of((spread, RANK, cut), BF16),
                shape_of((2 * tall, half_width + inner + 2 * RANK), BF16),
            ],
            [pltpu.VMEM((RANK, depth), BF16)],
        )
        handoff = swap(handoff, "tensor", 1)
        far, message, low = call(
            join_kernel,
            "join",
            [(VMEM, a) for a in (keep, low_keep, handoff)],
            [
                shape_of((tall, half_width), F32),
                shape_of((tall, half_width + 4 * RANK), BF16),
                shape_of((2 * tall, RANK), F32),
            ],
        )
        up_sets = {0: ups, 1: handoff}
    else:
        far_keep, far_got = reduce(keep, send)

        down_rows, ups = call(
            functools.partial(collect_kernel, slot=slot),
            "collect",
            [(ANY, keep)] + [(VMEM, factors[k]) for k in range(spread)],
            [shape_of((RANK, depth), BF16), shape_of((spread, RANK, cut), BF16)],
        )
        low_keep, low_send = call(
            lower_kernel,
            "lower",
            [(VMEM, a) for a in (*attended, down_rows)],
            [shape_of((sets * tall, RANK), F32), shape_of((sets * tall, 2 * RANK), BF16)],
        )
        low = reduce_low(low_keep, low_send)
        if ordered:
            ups = lax.all_gather(up, ("fsdp", "tensor"), axis=1, tiled=True)
            ups = ups.reshape(RANK, spread, 2, wide)
            top = lax.axis_index("tensor") // sets
            ups = lax.dynamic_index_in_dim(ups, top, 2, keepdims=False)
            up_sets = {0: ups.reshape(RANK, half_width)}
        else:
            up_sets = {0: ups}
            bit = sets // 2
            while bit:
                up_sets |= {k ^ bit: swap(u, "tensor", bit) for k, u in list(up_sets.items())}
                bit //= 2
        far = far_keep + far_got.astype(F32)
        low_parts = jnp.concatenate(split(low), axis=1)
        message = jnp.concatenate([far[tall:].astype(BF16), low_parts[tall:], low_parts[:tall]], axis=1)
        far = far[:tall]

    near = []

    def add_near(low, high, ahead):
        nonlocal buffers
        keep, send, buffers = project(attended, weight, buffers, low, high, ahead)
        near.append(reduce(keep, send))

    a, b = spread + quarter, 2 * spread - quarter
    add_near(spread, a, quarter)
    message, attended = lax.optimization_barrier((message, attended))
    message = swap(message, "tensor", sets)
    add_near(a, b, quarter)
    add_near(b, 2 * spread, 0)
    near_got, low_got = message[:, :half_width], message[:, half_width:]

    ups = [up_sets[k] for k in range(len(up_sets))]
    near_keep, near_send = call(
        functools.partial(adapt_kernel, pieces=len(near), sets=sets, ordered=ordered),
        "adapt",
        [(VMEM, a) for a in (low, low_got, *[k for k, _ in near], *[g for _, g in near], *ups)],
        [shape_of((tall, half_width), F32), shape_of((tall, half_width), BF16)],
        [pltpu.VMEM((2 * tall, half_width), F32)],
    )
    far_got = swap(near_send, "tensor", sets)

    return call(
        functools.partial(finish_kernel, own=own, steps=steps, strips=spread),
        "finish",
        [(VMEM, a) for a in (far, far_got, near_keep, near_got)],
        [shape_of((steps, own, weight.shape[1]), BF16)],
    )[0]


def solution(mesh):
    return jax.shard_map(
        shards,
        mesh=mesh,
        in_specs=(
            P(None, ("groups", "fsdp"), "tensor"),
            P(("groups", "fsdp", "tensor"), None, None, None, None),
            P(None, ("groups", "fsdp"), "tensor"),
            P(("groups", "fsdp", "tensor")),
            P("tensor", None),
            P("tensor", "fsdp"),
            P(None, ("fsdp", "tensor")),
        ),
        out_specs=P(None, ("groups", "fsdp", "tensor"), None),
        check_vma=False,
    )
```

```python
import functools

import jax
import jax.numpy as jnp
from jax import lax
from jax.experimental import pallas as pl
from jax.experimental.pallas import tpu as pltpu
from jax.sharding import PartitionSpec as P

HEADS = 64
KV_HEADS = 8
HEAD_DIM = 128
GROUP = HEADS // KV_HEADS
RANK = 64
LOG2_E = 1.4426950408889634
SCALE = 2.0
BF16 = jnp.bfloat16
F32 = jnp.float32
VMEM = pl.BlockSpec(memory_space=pltpu.VMEM)
ANY = pl.BlockSpec(memory_space=pl.ANY)
HBM = pl.BlockSpec(memory_space=pltpu.HBM)
ROW_ROW = (((1,), (1,)), ((), ()))
shape_of = jax.ShapeDtypeStruct


def dot(a, b):
    return jnp.dot(a, b, preferred_element_type=F32)


def dot_rows(a, b):
    return lax.dot_general(a, b, ROW_ROW, preferred_element_type=F32)


def call(kernel, name, ins, outs, scratch=(), mib=6, cost=None, alias=None):
    specs, args = zip(*ins)
    args = [
        pltpu.with_memory_space_constraint(a, pltpu.HBM) if s is HBM else a for s, a in ins
    ]
    return pl.pallas_call(
        kernel,
        in_specs=list(specs),
        out_specs=[VMEM] * len(outs),
        out_shape=list(outs),
        scratch_shapes=list(scratch),
        input_output_aliases=alias or {},
        compiler_params=pltpu.CompilerParams(vmem_limit_bytes=mib * 2**20),
        cost_estimate=cost,
        name=name,
    )(*args)


def split(x):
    high = x.astype(BF16)
    return high, (x - high.astype(F32)).astype(BF16)


def log2(n):
    return n.bit_length() - 1


def strip_copies(weight_hbm, strips_ref, sem, first):
    count, _, wide = strips_ref.shape
    spread = weight_hbm.shape[1] // (2 * wide)
    top = lax.axis_index("tensor") >> (log2(lax.axis_size("tensor")) - 1)
    copies = []
    for i in range(count):
        half = top if first + i >= spread else 1 - top
        start = pl.multiple_of((2 * ((first + i) % spread) + half) * wide, wide)
        copies.append(
            pltpu.make_async_copy(
                weight_hbm.at[:, pl.ds(start, wide)], strips_ref.at[i], sem.at[i]
            )
        )
    return copies


def stage_kernel(after_ref, cache_hbm, cache_ref, sem, *, own):
    slots = pl.ds(0, cache_hbm.shape[3])
    copies = [
        pltpu.make_async_copy(
            cache_hbm.at[r, part], cache_ref.at[r, part, :, slots], sem.at[r, part]
        )
        for r in range(own)
        for part in range(2)
    ]
    for copy in copies:
        copy.start()
    for copy in copies:
        copy.wait()


def pack_kernel(query_hbm, new_hbm, down_hbm, up_hbm, *refs, parts, own, steps):
    *block_refs, factor_ref, query_ref, new_ref, up_ref, sem = refs
    slot, depth = down_hbm.shape
    pairs = [
        (query_hbm, query_ref),
        (new_hbm, new_ref),
        (up_hbm, up_ref),
        (down_hbm, factor_ref.at[pl.ds(0, slot)]),
    ]
    copies = [pltpu.make_async_copy(*pair, sem.at[i]) for i, pair in enumerate(pairs)]
    for copy in copies:
        copy.start()
    me = lax.axis_index("tensor")
    count = steps * parts * own
    i = lax.broadcasted_iota(jnp.int32, (count, count), 0)
    j = lax.broadcasted_iota(jnp.int32, (count, count), 1)
    step_out = i & (steps - 1)
    row_out = (i >> log2(steps)) & (own - 1)
    part_out = (i >> log2(steps * own)) ^ me
    source = step_out * (parts * own) + part_out * own + row_out
    select = jnp.where(source == j, 1.0, 0.0).astype(BF16)
    for copy in copies[:3]:
        copy.wait()
    queries = dot(select, query_ref[...].reshape(count, query_ref.shape[2]))
    new = dot(select, new_ref[...].reshape(count, new_ref.shape[2]))
    heads = queries.shape[1] // HEAD_DIM
    pieces = new.shape[1] // HEAD_DIM
    tall = own * steps
    for k in range(parts):
        q = queries[k * tall : (k + 1) * tall]
        n = new[k * tall : (k + 1) * tall]
        tiles = [
            q[r * steps : (r + 1) * steps, h * HEAD_DIM : (h + 1) * HEAD_DIM]
            for r in range(own)
            for h in range(heads)
        ]
        tiles += [n[:, c * HEAD_DIM : (c + 1) * HEAD_DIM] for c in range(pieces)]
        block = jnp.concatenate(tiles, axis=0).astype(BF16)
        if k < parts // 2:
            block_refs[k][...] = block
        else:
            block_refs[-1][k - parts // 2] = block
    cut = up_ref.shape[1]
    per = depth // cut
    tall = RANK // per
    for c in range(per):
        factor_ref[slot : slot + tall, c * cut : (c + 1) * cut] = up_ref[c * tall : (c + 1) * tall, :]
    for copy in copies[3:]:
        copy.wait()


def attend_kernel(length_hbm, *refs, parts, own, steps):
    block_refs, refs = refs[:parts], refs[parts:]
    weight_hbm, refs = refs[0], refs[2:]
    out_refs, refs = refs[:parts], refs[parts:]
    strips_ref, cache_ref, length_ref, held_ref, attended_ref = refs[:5]
    scores_ref, weights_ref, mask_ref, length_sem, sem = refs[5:]
    length_copy = pltpu.make_async_copy(length_hbm, length_ref, length_sem)
    length_copy.start()
    heads = HEADS // parts
    pieces = 2 * KV_HEADS // parts
    query_rows = own * heads * steps
    tall = own * steps
    slots = cache_ref.shape[3] - tall
    count = GROUP * steps
    weight_copies = strip_copies(weight_hbm, strips_ref, sem, 0)
    for copy in weight_copies:
        copy.start()

    me = lax.axis_index("tensor")
    for k, block_ref in enumerate(block_refs):
        held_ref[me ^ k] = block_ref[0:query_rows, :]
        for c in range(pieces):
            piece = (me ^ k) * pieces + c
            start = query_rows + c * tall
            for r in range(own):
                cache_ref[r, piece >> log2(KV_HEADS), piece & (KV_HEADS - 1), slots : slots + tall, :] = (
                    block_ref[start : start + tall, :]
                )

    def queries(r, g):
        if heads >= GROUP:
            groups = heads // GROUP
            start = (r * heads + (g & (groups - 1)) * GROUP) * steps
            return held_ref[g >> log2(groups), pl.ds(pl.multiple_of(start, count), count), :]
        span = GROUP // heads
        start = pl.multiple_of(r * heads * steps, heads * steps)
        found = [held_ref[g * span + i, pl.ds(start, heads * steps), :] for i in range(span)]
        return jnp.concatenate(found, axis=0)

    slot = lax.broadcasted_iota(jnp.int32, (count, slots + tall), 1)
    step = lax.broadcasted_iota(jnp.int32, (count, slots + tall), 0) & (steps - 1)
    length_copy.wait()
    for r in range(own):
        fresh = slot - slots - r * steps
        valid = (slot < length_ref[r]) | ((fresh >= 0) & (fresh <= step))
        mask_ref[r] = jnp.where(valid, 0.0, -1e30)
    ones = jnp.ones((slots + tall, HEAD_DIM), BF16)

    def turn(i, _):
        scored = jnp.minimum(i, KV_HEADS - 1)
        summed = jnp.maximum(i - 2, 0)
        rows = range(own)
        mixed = [
            dot(weights_ref[r], jnp.concatenate([cache_ref[r, 1, summed], ones], axis=1)) for r in rows
        ]
        before = [scores_ref[r] for r in rows]
        weights = [jnp.exp2(b - b.max(-1, keepdims=True)) for b in before]
        scores = [
            dot_rows(queries(r, scored), cache_ref[r, 0, scored]) * (HEAD_DIM**-0.5 * LOG2_E)
            + mask_ref[r]
            for r in rows
        ]
        for r in rows:
            weights_ref[r] = jnp.concatenate(split(weights[r]), axis=0)
            scores_ref[r] = scores[r]
            total = mixed[r][:count] + mixed[r][count:]
            total = total[:, :HEAD_DIM] / total[:, HEAD_DIM:]
            for h in range(GROUP):
                head = summed * GROUP + h
                attended_ref[
                    head >> log2(heads), head & (heads - 1), pl.ds(r, steps, stride=own), :
                ] = total[h * steps : (h + 1) * steps]
        return 0

    lax.fori_loop(0, KV_HEADS + 2, turn, 0, unroll=2)
    for k in range(parts):
        for h in range(heads):
            out_refs[k][:, h * HEAD_DIM : (h + 1) * HEAD_DIM] = attended_ref[me ^ k, h].astype(BF16)
    for copy in weight_copies:
        copy.wait()


def collect_kernel(*refs, slot):
    _, *factor_refs, down_ref, up_ref = refs
    me = lax.axis_index("fsdp")
    cut = up_ref.shape[2]
    per = down_ref.shape[1] // cut
    tall = RANK // per
    for k, factor_ref in enumerate(factor_refs):
        down_ref[pl.ds(pl.multiple_of((me ^ k) * slot, slot), slot), :] = factor_ref[0:slot, :]
        for c in range(per):
            up_ref[k, c * tall : (c + 1) * tall, :] = factor_ref[
                slot : slot + tall, c * cut : (c + 1) * cut
            ]


def fetch_kernel(after_ref, weight_hbm, strips_ref, sem, *, first):
    copies = strip_copies(weight_hbm, strips_ref, sem, first)
    for copy in copies:
        copy.start()
    for copy in copies:
        copy.wait()


def project_kernel(*refs, parts, spans, ahead, first):
    attended_refs, refs = refs[:parts], refs[parts:]
    held_refs, refs = refs[: len(spans)], refs[len(spans) :]
    weight_hbm, keep_ref, send_ref, refs = refs[0], refs[1], refs[2], refs[3:]
    copies = []
    if ahead:
        ahead_ref, rows_ref, sem = refs
        copies = strip_copies(weight_hbm, ahead_ref, sem, first)
    else:
        rows_ref = refs[0]
    for copy in copies:
        copy.start()
    tall = attended_refs[0].shape[0]
    for k, attended_ref in enumerate(attended_refs):
        rows_ref[k * tall : (k + 1) * tall, :] = attended_ref[...]
    half = rows_ref.shape[0] // 2
    place = 0
    for strips_ref, (low, high) in zip(held_refs, spans):
        wide = strips_ref.shape[2]

        @pl.loop(low, high + jnp.minimum(lax.axis_index("tensor"), 0))
        def _(i, strips_ref=strips_ref, place=place - low):
            out = dot(rows_ref[...], strips_ref[i])
            lanes = pl.ds(pl.multiple_of((place + i) * wide, wide), wide)
            keep_ref[:, lanes] = out[:half]
            send_ref[:, lanes] = out[half:].astype(BF16)

        place += high - low
    for copy in copies:
        copy.wait()


def project(attended, weight, buffers, low, high, ahead=0):
    parts = len(attended)
    tall, depth = attended[0].shape
    half = parts * tall // 2
    held, spans = [], []
    for first, buffer in buffers:
        a, b = max(low - first, 0), min(high - first, buffer.shape[0])
        if a < b:
            held.append(buffer)
            spans.append((a, b))
    wide = held[0].shape[2]
    width = wide * (high - low)
    next_strip = buffers[-1][0] + buffers[-1][1].shape[0]
    outs = [shape_of((half, width), F32), shape_of((half, width), BF16)]
    ins = [(VMEM, a) for a in attended] + [(VMEM, h) for h in held] + [(HBM, weight)]
    scratch = [pltpu.VMEM((parts * tall, depth), BF16)]
    if ahead:
        outs += [pltpu.VMEM((ahead, depth, wide), BF16)]
        scratch += [pltpu.SemaphoreType.DMA((ahead,))]
    kernel = functools.partial(
        project_kernel, parts=parts, spans=spans, ahead=ahead, first=next_strip
    )
    cost = pl.CostEstimate(
        flops=2 * parts * tall * depth * width, bytes_accessed=2 * depth * width, transcendentals=0
    )
    keep, send, *rest = call(kernel, "project", ins, outs, scratch, cost=cost)
    return keep, send, buffers + [(next_strip, rest[0])] if ahead else buffers


def lower_kernel(*refs):
    *attended_refs, down_ref, keep_ref, send_ref = refs
    half = len(attended_refs) // 2
    for first, last in ((0, half), (half, 2 * half)):
        rows = jnp.concatenate([a[...] for a in attended_refs[first:last]], axis=0)
        low = dot_rows(rows, down_ref[...])
        if first:
            send_ref[...] = jnp.concatenate(split(low), axis=1)
        else:
            keep_ref[...] = low


def handoff_kernel(send_ref, *refs, parts, slot):
    attended_refs, refs = refs[:parts], refs[parts:]
    *factor_refs, keep_ref, up_ref, handoff_ref, down_ref = refs
    collect_kernel(None, *factor_refs, down_ref, up_ref, slot=slot)
    half, width = send_ref.shape
    handoff_ref[:, :width] = send_ref[...]
    cut = up_ref.shape[2]
    for k in range(up_ref.shape[0]):
        for j in range(RANK // half):
            handoff_ref[:, width : width + cut] = up_ref[k, j * half : (j + 1) * half, :]
            width += cut
    rows = [
        jnp.concatenate([a[...] for a in attended_refs[i : i + parts // 2]], axis=0)
        for i in (0, parts // 2)
    ]
    keep_ref[...] = dot_rows(rows[0], down_ref[...])
    handoff_ref[:, width:] = jnp.concatenate(split(dot_rows(rows[1], down_ref[...])), axis=1)


def fold_low(keep, got):
    return keep + got[:, :RANK].astype(F32) + got[:, RANK:].astype(F32)


def adapt_kernel(*refs, pieces, sets, ordered):
    low_ref, low_got_ref, refs = refs[0], refs[1], refs[2:]
    keep_refs, refs = refs[:pieces], refs[pieces:]
    got_refs, refs = refs[:pieces], refs[pieces:]
    *up_refs, own_ref, send_ref, extra_ref = refs
    me, place = lax.axis_index("tensor"), lax.axis_index("fsdp")
    half = low_ref.shape[0] // 2
    got = low_got_ref[...]
    got = jnp.concatenate([got[:, : 2 * RANK], got[:, 2 * RANK :]], axis=0)
    low = SCALE * fold_low(low_ref[...], got)
    low = jnp.concatenate(split(low), axis=0)
    if ordered:
        both = dot(low, up_refs[0][...])
        extra_ref[...] = both[: 2 * half] + both[2 * half :]
    else:
        spread, _, cut = up_refs[0].shape
        for kt in range(sets):
            for kf in range(spread):
                if kt < len(up_refs) and len(up_refs[kt].shape) == 3:
                    factor = up_refs[kt][kf]
                else:
                    tall = up_refs[kt].shape[0]
                    first = extra_ref.shape[1] + kf * (RANK // tall) * cut
                    factor = jnp.concatenate(
                        [
                            up_refs[kt][:, first + j * cut : first + (j + 1) * cut]
                            for j in range(RANK // tall)
                        ],
                        axis=0,
                    )
                both = dot(low, factor)
                column = (place ^ kf) * sets + ((me ^ kt) & (sets - 1))
                start = pl.multiple_of(column * cut, cut)
                extra_ref[:, pl.ds(start, cut)] = both[: 2 * half] + both[2 * half :]
    first = 0
    for keep_ref, got_ref in zip(keep_refs, got_refs):
        lanes = slice(first, first + keep_ref.shape[1])
        first += keep_ref.shape[1]
        total = keep_ref[...] + got_ref[...].astype(F32) + extra_ref[:, lanes]
        own_ref[:, lanes] = total[:half]
        send_ref[:, lanes] = total[half:].astype(BF16)


def join_kernel(keep_ref, low_keep_ref, handoff_ref, own_ref, message_ref, low_ref):
    half, width = own_ref.shape
    own_ref[...] = keep_ref[:half, :] + handoff_ref[:half, :width].astype(F32)
    total = keep_ref[half:, :] + handoff_ref[half:, :width].astype(F32)
    message_ref[:, :width] = total.astype(BF16)
    low = fold_low(low_keep_ref[...], handoff_ref[:, handoff_ref.shape[1] - 2 * RANK :])
    low_ref[...] = low
    parts = jnp.concatenate(split(low), axis=1)
    message_ref[:, width:] = jnp.concatenate([parts[half:], parts[:half]], axis=1)


def finish_kernel(far_ref, far_got_ref, near_ref, near_got_ref, out_ref, *, own, steps, strips):
    top = lax.axis_index("tensor") >> (log2(lax.axis_size("tensor")) - 1)
    wide = near_ref.shape[1] // strips
    for keep_ref, got_ref, half in ((near_ref, near_got_ref, top), (far_ref, far_got_ref, 1 - top)):
        for i in range(strips):
            lanes = slice(i * wide, (i + 1) * wide)
            total = (keep_ref[:, lanes] + got_ref[:, lanes].astype(F32)).astype(BF16)
            start = pl.multiple_of((2 * i + half) * wide, wide)
            out_ref[:, :, pl.ds(start, wide)] = total.reshape(steps, own, wide)


def shards(queries, cache, new, lengths, weight, down, up):
    parts, spread = lax.axis_size("tensor"), lax.axis_size("fsdp")
    steps, rows, width = queries.shape
    own = rows // parts
    tall = own * steps
    depth, slot = down.shape
    cut = up.shape[1]
    heads, pieces = width // HEAD_DIM, new.shape[2] // HEAD_DIM
    sets = parts // 2
    wide = sets * cut
    half_width = spread * wide
    swap = lambda x, axis, k: lax.ppermute(
        x, axis, [(i, i ^ k) for i in range(lax.axis_size(axis))]
    )

    block = shape_of((own * heads * steps + pieces * tall, HEAD_DIM), BF16)
    per = depth // cut
    *blocks, cross, factors = call(
        functools.partial(pack_kernel, parts=parts, own=own, steps=steps),
        "pack",
        [(HBM, a) for a in (queries, new, down.T, up)],
        [block] * sets
        + [shape_of((sets,) + block.shape, BF16), shape_of((slot + RANK // per, depth), BF16)],
        [
            pltpu.VMEM(queries.shape, BF16),
            pltpu.VMEM(new.shape, BF16),
            pltpu.VMEM(up.shape, BF16),
            pltpu.SemaphoreType.DMA((4,)),
        ],
    )
    (cache,) = call(
        functools.partial(stage_kernel, own=own),
        "stage",
        [(ANY, blocks[0]), (HBM, cache)],
        [pltpu.VMEM(cache.shape[:3] + (cache.shape[3] + tall, HEAD_DIM), BF16)],
        [pltpu.SemaphoreType.DMA((own, 2))],
        cost=pl.CostEstimate(flops=0, bytes_accessed=2 * cache.size, transcendentals=0),
    )
    cross = swap(cross, "tensor", sets)
    cross, cache = lax.optimization_barrier((cross, cache))
    blocks = blocks[:1] + [swap(blocks[k], "tensor", k) for k in range(1, sets)]
    blocks += [cross[0]] + [swap(cross[k], "tensor", k) for k in range(1, sets)]
    factors = {0: factors}
    bit = spread // 2
    while bit > 1:
        factors |= {k ^ bit: swap(v, "fsdp", bit) for k, v in list(factors.items())}
        bit //= 2

    half, quarter = spread // 2, spread // 4
    early = half
    fetched = half
    attended = call(
        functools.partial(attend_kernel, parts=parts, own=own, steps=steps),
        "attend",
        [(HBM, lengths)] + [(VMEM, b) for b in blocks] + [(HBM, weight), (VMEM, cache)],
        [shape_of((tall, width), BF16)] * parts
        + [pltpu.VMEM((early, depth, wide), BF16), pltpu.VMEM(cache.shape, BF16)],
        [
            pltpu.SMEM(lengths.shape, jnp.int32),
            pltpu.VMEM((parts, own * heads * steps, HEAD_DIM), BF16),
            pltpu.VMEM((parts, heads, tall, HEAD_DIM), F32),
            pltpu.VMEM((own, GROUP * steps, cache.shape[3]), F32),
            pltpu.VMEM((own, 2 * GROUP * steps, cache.shape[3]), BF16),
            pltpu.VMEM((own, GROUP * steps, cache.shape[3]), F32),
            pltpu.SemaphoreType.DMA(()),
            pltpu.SemaphoreType.DMA((early,)),
        ],
        alias={parts + 2: parts + 1},
    )
    attended, buffers = attended[:parts], [(0, attended[parts])]
    buffers += [
        (
            early,
            call(
                functools.partial(fetch_kernel, first=early),
                "fetch",
                [(ANY, attended[0]), (HBM, weight)],
                [pltpu.VMEM((fetched, depth, wide), BF16)],
                [pltpu.SemaphoreType.DMA((fetched,))],
                cost=pl.CostEstimate(
                    flops=0, bytes_accessed=2 * fetched * depth * wide, transcendentals=0
                ),
            )[0],
        )
    ]
    attended, factors = lax.optimization_barrier((list(attended), factors))
    factors |= {k ^ 1: swap(v, "fsdp", 1) for k, v in list(factors.items())}
    got = {k: swap(attended[k], "tensor", k) for k in range(parts - 1, 0, -1)}
    attended = [attended[0]] + [got[k] for k in range(1, parts)]

    order = sorted(range(parts), key=lambda k: format(k, "08b")[::-1])
    attended = [attended[k] for k in order]

    def reduce(keep, send):
        bit = 1
        while True:
            got = swap(send, "tensor", bit)
            bit *= 2
            if bit == sets:
                return keep, got
            both = keep + got.astype(F32)
            half = both.shape[0] // 2
            keep, send = both[:half], both[half:].astype(BF16)

    def reduce_low(keep, send):
        bit = 1
        while True:
            both = fold_low(keep, swap(send, "tensor", bit))
            bit *= 2
            if bit == sets:
                return both
            half = both.shape[0] // 2
            keep, send = both[:half], jnp.concatenate(split(both[half:]), axis=1)

    keep, send, buffers = project(attended, weight, buffers, 0, spread, half)
    ordered = cut % HEAD_DIM != 0
    if sets == 2 and not ordered:
        inner = (spread * RANK * cut) // (2 * tall)
        low_keep, ups, handoff = call(
            functools.partial(handoff_kernel, parts=parts, slot=slot),
            "handoff",
            [(VMEM, a) for a in (send, *attended, *[factors[k] for k in range(spread)])],
            [
                shape_of((2 * tall, RANK), F32),
                shape_of((spread, RANK, cut), BF16),
                shape_of((2 * tall, half_width + inner + 2 * RANK), BF16),
            ],
            [pltpu.VMEM((RANK, depth), BF16)],
        )
        handoff = swap(handoff, "tensor", 1)
        far, message, low = call(
            join_kernel,
            "join",
            [(VMEM, a) for a in (keep, low_keep, handoff)],
            [
                shape_of((tall, half_width), F32),
                shape_of((tall, half_width + 4 * RANK), BF16),
                shape_of((2 * tall, RANK), F32),
            ],
        )
        up_sets = {0: ups, 1: handoff}
    else:
        far_keep, far_got = reduce(keep, send)

        down_rows, ups = call(
            functools.partial(collect_kernel, slot=slot),
            "collect",
            [(ANY, keep)] + [(VMEM, factors[k]) for k in range(spread)],
            [shape_of((RANK, depth), BF16), shape_of((spread, RANK, cut), BF16)],
        )
        low_keep, low_send = call(
            lower_kernel,
            "lower",
            [(VMEM, a) for a in (*attended, down_rows)],
            [shape_of((sets * tall, RANK), F32), shape_of((sets * tall, 2 * RANK), BF16)],
        )
        low = reduce_low(low_keep, low_send)
        if ordered:
            ups = lax.all_gather(up, ("fsdp", "tensor"), axis=1, tiled=True)
            ups = ups.reshape(RANK, spread, 2, wide)
            top = lax.axis_index("tensor") // sets
            ups = lax.dynamic_index_in_dim(ups, top, 2, keepdims=False)
            up_sets = {0: ups.reshape(RANK, half_width)}
        else:
            up_sets = {0: ups}
            bit = sets // 2
            while bit:
                up_sets |= {k ^ bit: swap(u, "tensor", bit) for k, u in list(up_sets.items())}
                bit //= 2
        far = far_keep + far_got.astype(F32)
        low_parts = jnp.concatenate(split(low), axis=1)
        message = jnp.concatenate([far[tall:].astype(BF16), low_parts[tall:], low_parts[:tall]], axis=1)
        far = far[:tall]

    near = []

    def add_near(low, high, ahead):
        nonlocal buffers
        keep, send, buffers = project(attended, weight, buffers, low, high, ahead)
        near.append(reduce(keep, send))

    a, b = spread + quarter, 2 * spread - quarter
    add_near(spread, a, quarter)
    message, attended = lax.optimization_barrier((message, attended))
    message = swap(message, "tensor", sets)
    add_near(a, b, quarter)
    add_near(b, 2 * spread, 0)
    near_got, low_got = message[:, :half_width], message[:, half_width:]

    ups = [up_sets[k] for k in range(len(up_sets))]
    near_keep, near_send = call(
        functools.partial(adapt_kernel, pieces=len(near), sets=sets, ordered=ordered),
        "adapt",
        [(VMEM, a) for a in (low, low_got, *[k for k, _ in near], *[g for _, g in near], *ups)],
        [shape_of((tall, half_width), F32), shape_of((tall, half_width), BF16)],
        [pltpu.VMEM((2 * tall, half_width), F32)],
    )
    far_got = swap(near_send, "tensor", sets)

    return call(
        functools.partial(finish_kernel, own=own, steps=steps, strips=spread),
        "finish",
        [(VMEM, a) for a in (far, far_got, near_keep, near_got)],
        [shape_of((steps, own, weight.shape[1]), BF16)],
    )[0]


def solution(mesh):
    return jax.shard_map(
        shards,
        mesh=mesh,
        in_specs=(
            P(None, ("groups", "fsdp"), "tensor"),
            P(("groups", "fsdp", "tensor"), None, None, None, None),
            P(None, ("groups", "fsdp"), "tensor"),
            P(("groups", "fsdp", "tensor")),
            P("tensor", None),
            P("tensor", "fsdp"),
            P(None, ("fsdp", "tensor")),
        ),
        out_specs=P(None, ("groups", "fsdp", "tensor"), None),
        check_vma=False,
    )
```

```python
import functools

import jax
import jax.numpy as jnp
from jax import lax
from jax.experimental import pallas as pl
from jax.experimental.pallas import tpu as pltpu
from jax.sharding import PartitionSpec as P

HEADS = 64
KV_HEADS = 8
HEAD_DIM = 128
GROUP = HEADS // KV_HEADS
RANK = 64
LOG2_E = 1.4426950408889634
SCALE = 2.0
BF16 = jnp.bfloat16
F32 = jnp.float32
VMEM = pl.BlockSpec(memory_space=pltpu.VMEM)
ANY = pl.BlockSpec(memory_space=pl.ANY)
HBM = pl.BlockSpec(memory_space=pltpu.HBM)
ROW_ROW = (((1,), (1,)), ((), ()))
shape_of = jax.ShapeDtypeStruct


def dot(a, b):
    return jnp.dot(a, b, preferred_element_type=F32)


def dot_rows(a, b):
    return lax.dot_general(a, b, ROW_ROW, preferred_element_type=F32)


def call(kernel, name, ins, outs, scratch=(), mib=6, cost=None, alias=None):
    specs, args = zip(*ins)
    args = [
        pltpu.with_memory_space_constraint(a, pltpu.HBM) if s is HBM else a for s, a in ins
    ]
    return pl.pallas_call(
        kernel,
        in_specs=list(specs),
        out_specs=[VMEM] * len(outs),
        out_shape=list(outs),
        scratch_shapes=list(scratch),
        input_output_aliases=alias or {},
        compiler_params=pltpu.CompilerParams(vmem_limit_bytes=mib * 2**20),
        cost_estimate=cost,
        name=name,
    )(*args)


def split(x):
    high = x.astype(BF16)
    return high, (x - high.astype(F32)).astype(BF16)


def log2(n):
    return n.bit_length() - 1


def strip_copies(weight_hbm, strips_ref, sem, first):
    count, _, wide = strips_ref.shape
    spread = weight_hbm.shape[1] // (2 * wide)
    top = lax.axis_index("tensor") >> (log2(lax.axis_size("tensor")) - 1)
    copies = []
    for i in range(count):
        half = top if first + i >= spread else 1 - top
        start = pl.multiple_of((2 * ((first + i) % spread) + half) * wide, wide)
        copies.append(
            pltpu.make_async_copy(
                weight_hbm.at[:, pl.ds(start, wide)], strips_ref.at[i], sem.at[i]
            )
        )
    return copies


def stage_kernel(after_ref, cache_hbm, cache_ref, sem, *, own):
    slots = pl.ds(0, cache_hbm.shape[3])
    copies = [
        pltpu.make_async_copy(
            cache_hbm.at[r, part], cache_ref.at[r, part, :, slots], sem.at[r, part]
        )
        for r in range(own)
        for part in range(2)
    ]
    for copy in copies:
        copy.start()
    for copy in copies:
        copy.wait()


def pack_kernel(query_hbm, new_hbm, down_hbm, up_hbm, length_hbm, *refs, parts, own, steps):
    *block_refs, factor_ref, limit_ref, query_ref, new_ref, up_ref, length_ref, sem = refs
    slot, depth = down_hbm.shape
    pairs = [
        (query_hbm, query_ref),
        (new_hbm, new_ref),
        (length_hbm, length_ref),
        (up_hbm, up_ref),
        (down_hbm, factor_ref.at[pl.ds(0, slot)]),
    ]
    copies = [pltpu.make_async_copy(*pair, sem.at[i]) for i, pair in enumerate(pairs)]
    for copy in copies:
        copy.start()
    me = lax.axis_index("tensor")
    count = steps * parts * own
    i = lax.broadcasted_iota(jnp.int32, (count, count), 0)
    j = lax.broadcasted_iota(jnp.int32, (count, count), 1)
    step_out = i & (steps - 1)
    row_out = (i >> log2(steps)) & (own - 1)
    part_out = (i >> log2(steps * own)) ^ me
    source = step_out * (parts * own) + part_out * own + row_out
    select = jnp.where(source == j, 1.0, 0.0).astype(BF16)
    for copy in copies[:4]:
        copy.wait()
    for r in range(own):
        limit_ref[r] = jnp.full(limit_ref.shape[1:], length_ref[r], jnp.int32)
    queries = dot(select, query_ref[...].reshape(count, query_ref.shape[2]))
    new = dot(select, new_ref[...].reshape(count, new_ref.shape[2]))
    heads = queries.shape[1] // HEAD_DIM
    pieces = new.shape[1] // HEAD_DIM
    tall = own * steps
    for k in range(parts):
        q = queries[k * tall : (k + 1) * tall]
        n = new[k * tall : (k + 1) * tall]
        tiles = [
            q[r * steps : (r + 1) * steps, h * HEAD_DIM : (h + 1) * HEAD_DIM]
            for r in range(own)
            for h in range(heads)
        ]
        tiles += [n[:, c * HEAD_DIM : (c + 1) * HEAD_DIM] for c in range(pieces)]
        block = jnp.concatenate(tiles, axis=0).astype(BF16)
        if k < parts // 2:
            block_refs[k][...] = block
        else:
            block_refs[-1][k - parts // 2] = block
    cut = up_ref.shape[1]
    per = depth // cut
    tall = RANK // per
    for c in range(per):
        factor_ref[slot : slot + tall, c * cut : (c + 1) * cut] = up_ref[c * tall : (c + 1) * tall, :]
    for copy in copies[4:]:
        copy.wait()


def attend_kernel(limit_ref, *refs, parts, own, steps):
    block_refs, refs = refs[:parts], refs[parts:]
    weight_hbm, refs = refs[0], refs[2:]
    out_refs, refs = refs[:parts], refs[parts:]
    strips_ref, cache_ref, held_ref, attended_ref = refs[:4]
    scores_ref, weights_ref, mask_ref, sem = refs[4:]
    heads = HEADS // parts
    pieces = 2 * KV_HEADS // parts
    query_rows = own * heads * steps
    tall = own * steps
    slots = cache_ref.shape[3] - tall
    count = GROUP * steps
    weight_copies = strip_copies(weight_hbm, strips_ref, sem, 0)
    for copy in weight_copies:
        copy.start()

    me = lax.axis_index("tensor")
    for k, block_ref in enumerate(block_refs):
        held_ref[me ^ k] = block_ref[0:query_rows, :]
        for c in range(pieces):
            piece = (me ^ k) * pieces + c
            start = query_rows + c * tall
            for r in range(own):
                cache_ref[r, piece >> log2(KV_HEADS), piece & (KV_HEADS - 1), slots : slots + tall, :] = (
                    block_ref[start : start + tall, :]
                )

    def queries(r, g):
        if heads >= GROUP:
            groups = heads // GROUP
            start = (r * heads + (g & (groups - 1)) * GROUP) * steps
            return held_ref[g >> log2(groups), pl.ds(pl.multiple_of(start, count), count), :]
        span = GROUP // heads
        start = pl.multiple_of(r * heads * steps, heads * steps)
        found = [held_ref[g * span + i, pl.ds(start, heads * steps), :] for i in range(span)]
        return jnp.concatenate(found, axis=0)

    slot = lax.broadcasted_iota(jnp.int32, (count, slots + tall), 1)
    step = lax.broadcasted_iota(jnp.int32, (count, slots + tall), 0) & (steps - 1)
    for r in range(own):
        limit = jnp.concatenate([limit_ref[r]] * GROUP, axis=0)
        limit = jnp.concatenate([limit] * (-(-(slots + tall) // HEAD_DIM)), axis=1)
        limit = limit[:, : slots + tall]
        fresh = slot - slots - r * steps
        valid = (slot < limit) | ((fresh >= 0) & (fresh <= step))
        mask_ref[r] = jnp.where(valid, 0.0, -1e30)
    ones = jnp.ones((slots + tall, HEAD_DIM), BF16)

    def turn(i, _):
        scored = jnp.minimum(i, KV_HEADS - 1)
        summed = jnp.maximum(i - 2, 0)
        rows = range(own)
        mixed = [
            dot(weights_ref[r], jnp.concatenate([cache_ref[r, 1, summed], ones], axis=1)) for r in rows
        ]
        before = [scores_ref[r] for r in rows]
        weights = [jnp.exp2(b - b.max(-1, keepdims=True)) for b in before]
        scores = [
            dot_rows(queries(r, scored), cache_ref[r, 0, scored]) * (HEAD_DIM**-0.5 * LOG2_E)
            + mask_ref[r]
            for r in rows
        ]
        for r in rows:
            weights_ref[r] = jnp.concatenate(split(weights[r]), axis=0)
            scores_ref[r] = scores[r]
            total = mixed[r][:count] + mixed[r][count:]
            total = total[:, :HEAD_DIM] / total[:, HEAD_DIM:]
            for h in range(GROUP):
                head = summed * GROUP + h
                attended_ref[
                    head >> log2(heads), head & (heads - 1), pl.ds(r, steps, stride=own), :
                ] = total[h * steps : (h + 1) * steps]
        return 0

    lax.fori_loop(0, KV_HEADS + 2, turn, 0, unroll=2)
    for k in range(parts):
        for h in range(heads):
            out_refs[k][:, h * HEAD_DIM : (h + 1) * HEAD_DIM] = attended_ref[me ^ k, h].astype(BF16)
    for copy in weight_copies:
        copy.wait()


def collect_kernel(*refs, slot):
    _, *factor_refs, down_ref, up_ref = refs
    me = lax.axis_index("fsdp")
    cut = up_ref.shape[2]
    per = down_ref.shape[1] // cut
    tall = RANK // per
    for k, factor_ref in enumerate(factor_refs):
        down_ref[pl.ds(pl.multiple_of((me ^ k) * slot, slot), slot), :] = factor_ref[0:slot, :]
        for c in range(per):
            up_ref[k, c * tall : (c + 1) * tall, :] = factor_ref[
                slot : slot + tall, c * cut : (c + 1) * cut
            ]


def fetch_kernel(after_ref, weight_hbm, strips_ref, sem, *, first):
    copies = strip_copies(weight_hbm, strips_ref, sem, first)
    for copy in copies:
        copy.start()
    for copy in copies:
        copy.wait()


def project_kernel(*refs, parts, spans, ahead, first):
    attended_refs, refs = refs[:parts], refs[parts:]
    held_refs, refs = refs[: len(spans)], refs[len(spans) :]
    weight_hbm, keep_ref, send_ref, refs = refs[0], refs[1], refs[2], refs[3:]
    copies = []
    if ahead:
        ahead_ref, rows_ref, sem = refs
        copies = strip_copies(weight_hbm, ahead_ref, sem, first)
    else:
        rows_ref = refs[0]
    for copy in copies:
        copy.start()
    tall = attended_refs[0].shape[0]
    for k, attended_ref in enumerate(attended_refs):
        rows_ref[k * tall : (k + 1) * tall, :] = attended_ref[...]
    half = rows_ref.shape[0] // 2
    place = 0
    for strips_ref, (low, high) in zip(held_refs, spans):
        wide = strips_ref.shape[2]

        @pl.loop(low, high + jnp.minimum(lax.axis_index("tensor"), 0))
        def _(i, strips_ref=strips_ref, place=place - low):
            out = dot(rows_ref[...], strips_ref[i])
            lanes = pl.ds(pl.multiple_of((place + i) * wide, wide), wide)
            keep_ref[:, lanes] = out[:half]
            send_ref[:, lanes] = out[half:].astype(BF16)

        place += high - low
    for copy in copies:
        copy.wait()


def project(attended, weight, buffers, low, high, ahead=0):
    parts = len(attended)
    tall, depth = attended[0].shape
    half = parts * tall // 2
    held, spans = [], []
    for first, buffer in buffers:
        a, b = max(low - first, 0), min(high - first, buffer.shape[0])
        if a < b:
            held.append(buffer)
            spans.append((a, b))
    wide = held[0].shape[2]
    width = wide * (high - low)
    next_strip = buffers[-1][0] + buffers[-1][1].shape[0]
    outs = [shape_of((half, width), F32), shape_of((half, width), BF16)]
    ins = [(VMEM, a) for a in attended] + [(VMEM, h) for h in held] + [(HBM, weight)]
    scratch = [pltpu.VMEM((parts * tall, depth), BF16)]
    if ahead:
        outs += [pltpu.VMEM((ahead, depth, wide), BF16)]
        scratch += [pltpu.SemaphoreType.DMA((ahead,))]
    kernel = functools.partial(
        project_kernel, parts=parts, spans=spans, ahead=ahead, first=next_strip
    )
    cost = pl.CostEstimate(
        flops=2 * parts * tall * depth * width, bytes_accessed=2 * depth * width, transcendentals=0
    )
    keep, send, *rest = call(kernel, "project", ins, outs, scratch, cost=cost)
    return keep, send, buffers + [(next_strip, rest[0])] if ahead else buffers


def lower_kernel(*refs):
    *attended_refs, down_ref, keep_ref, send_ref = refs
    half = len(attended_refs) // 2
    for first, last in ((0, half), (half, 2 * half)):
        rows = jnp.concatenate([a[...] for a in attended_refs[first:last]], axis=0)
        low = dot_rows(rows, down_ref[...])
        if first:
            send_ref[...] = jnp.concatenate(split(low), axis=1)
        else:
            keep_ref[...] = low


def handoff_kernel(send_ref, *refs, parts, slot):
    attended_refs, refs = refs[:parts], refs[parts:]
    *factor_refs, keep_ref, up_ref, handoff_ref, down_ref = refs
    collect_kernel(None, *factor_refs, down_ref, up_ref, slot=slot)
    half, width = send_ref.shape
    handoff_ref[:, :width] = send_ref[...]
    cut = up_ref.shape[2]
    for k in range(up_ref.shape[0]):
        for j in range(RANK // half):
            handoff_ref[:, width : width + cut] = up_ref[k, j * half : (j + 1) * half, :]
            width += cut
    rows = [
        jnp.concatenate([a[...] for a in attended_refs[i : i + parts // 2]], axis=0)
        for i in (0, parts // 2)
    ]
    keep_ref[...] = dot_rows(rows[0], down_ref[...])
    handoff_ref[:, width:] = jnp.concatenate(split(dot_rows(rows[1], down_ref[...])), axis=1)


def fold_low(keep, got):
    return keep + got[:, :RANK].astype(F32) + got[:, RANK:].astype(F32)


def adapt_kernel(*refs, pieces, sets, ordered):
    low_ref, low_got_ref, refs = refs[0], refs[1], refs[2:]
    keep_refs, refs = refs[:pieces], refs[pieces:]
    got_refs, refs = refs[:pieces], refs[pieces:]
    *up_refs, own_ref, send_ref, extra_ref = refs
    me, place = lax.axis_index("tensor"), lax.axis_index("fsdp")
    half = low_ref.shape[0] // 2
    got = low_got_ref[...]
    got = jnp.concatenate([got[:, : 2 * RANK], got[:, 2 * RANK :]], axis=0)
    low = SCALE * fold_low(low_ref[...], got)
    low = jnp.concatenate(split(low), axis=0)
    if ordered:
        both = dot(low, up_refs[0][...])
        extra_ref[...] = both[: 2 * half] + both[2 * half :]
    else:
        spread, _, cut = up_refs[0].shape
        for kt in range(sets):
            for kf in range(spread):
                if kt < len(up_refs) and len(up_refs[kt].shape) == 3:
                    factor = up_refs[kt][kf]
                else:
                    tall = up_refs[kt].shape[0]
                    first = extra_ref.shape[1] + kf * (RANK // tall) * cut
                    factor = jnp.concatenate(
                        [
                            up_refs[kt][:, first + j * cut : first + (j + 1) * cut]
                            for j in range(RANK // tall)
                        ],
                        axis=0,
                    )
                both = dot(low, factor)
                column = (place ^ kf) * sets + ((me ^ kt) & (sets - 1))
                start = pl.multiple_of(column * cut, cut)
                extra_ref[:, pl.ds(start, cut)] = both[: 2 * half] + both[2 * half :]
    first = 0
    for keep_ref, got_ref in zip(keep_refs, got_refs):
        lanes = slice(first, first + keep_ref.shape[1])
        first += keep_ref.shape[1]
        total = keep_ref[...] + got_ref[...].astype(F32) + extra_ref[:, lanes]
        own_ref[:, lanes] = total[:half]
        send_ref[:, lanes] = total[half:].astype(BF16)


def join_kernel(keep_ref, low_keep_ref, handoff_ref, own_ref, message_ref, low_ref):
    half, width = own_ref.shape
    own_ref[...] = keep_ref[:half, :] + handoff_ref[:half, :width].astype(F32)
    total = keep_ref[half:, :] + handoff_ref[half:, :width].astype(F32)
    message_ref[:, :width] = total.astype(BF16)
    low = fold_low(low_keep_ref[...], handoff_ref[:, handoff_ref.shape[1] - 2 * RANK :])
    low_ref[...] = low
    parts = jnp.concatenate(split(low), axis=1)
    message_ref[:, width:] = jnp.concatenate([parts[half:], parts[:half]], axis=1)


def finish_kernel(far_ref, far_got_ref, near_ref, near_got_ref, out_ref, *, own, steps, strips):
    top = lax.axis_index("tensor") >> (log2(lax.axis_size("tensor")) - 1)
    wide = near_ref.shape[1] // strips
    for keep_ref, got_ref, half in ((near_ref, near_got_ref, top), (far_ref, far_got_ref, 1 - top)):
        for i in range(strips):
            lanes = slice(i * wide, (i + 1) * wide)
            total = (keep_ref[:, lanes] + got_ref[:, lanes].astype(F32)).astype(BF16)
            start = pl.multiple_of((2 * i + half) * wide, wide)
            out_ref[:, :, pl.ds(start, wide)] = total.reshape(steps, own, wide)


def shards(queries, cache, new, lengths, weight, down, up):
    parts, spread = lax.axis_size("tensor"), lax.axis_size("fsdp")
    steps, rows, width = queries.shape
    own = rows // parts
    tall = own * steps
    depth, slot = down.shape
    cut = up.shape[1]
    heads, pieces = width // HEAD_DIM, new.shape[2] // HEAD_DIM
    sets = parts // 2
    wide = sets * cut
    half_width = spread * wide
    swap = lambda x, axis, k: lax.ppermute(
        x, axis, [(i, i ^ k) for i in range(lax.axis_size(axis))]
    )

    block = shape_of((own * heads * steps + pieces * tall, HEAD_DIM), BF16)
    per = depth // cut
    *blocks, cross, factors, limits = call(
        functools.partial(pack_kernel, parts=parts, own=own, steps=steps),
        "pack",
        [(HBM, a) for a in (queries, new, down.T, up, lengths)],
        [block] * sets
        + [
            shape_of((sets,) + block.shape, BF16),
            shape_of((slot + RANK // per, depth), BF16),
            shape_of((own, steps, HEAD_DIM), jnp.int32),
        ],
        [
            pltpu.VMEM(queries.shape, BF16),
            pltpu.VMEM(new.shape, BF16),
            pltpu.VMEM(up.shape, BF16),
            pltpu.SMEM(lengths.shape, jnp.int32),
            pltpu.SemaphoreType.DMA((5,)),
        ],
    )
    (cache,) = call(
        functools.partial(stage_kernel, own=own),
        "stage",
        [(ANY, blocks[0]), (HBM, cache)],
        [pltpu.VMEM(cache.shape[:3] + (cache.shape[3] + tall, HEAD_DIM), BF16)],
        [pltpu.SemaphoreType.DMA((own, 2))],
        cost=pl.CostEstimate(flops=0, bytes_accessed=2 * cache.size, transcendentals=0),
    )
    cross = swap(cross, "tensor", sets)
    cross, cache = lax.optimization_barrier((cross, cache))
    blocks = blocks[:1] + [swap(blocks[k], "tensor", k) for k in range(1, sets)]
    blocks += [cross[0]] + [swap(cross[k], "tensor", k) for k in range(1, sets)]
    factors = {0: factors}
    bit = spread // 2
    while bit > 1:
        factors |= {k ^ bit: swap(v, "fsdp", bit) for k, v in list(factors.items())}
        bit //= 2

    half, quarter = spread // 2, spread // 4
    early = half
    fetched = half
    attended = call(
        functools.partial(attend_kernel, parts=parts, own=own, steps=steps),
        "attend",
        [(VMEM, limits)] + [(VMEM, b) for b in blocks] + [(HBM, weight), (VMEM, cache)],
        [shape_of((tall, width), BF16)] * parts
        + [pltpu.VMEM((early, depth, wide), BF16), pltpu.VMEM(cache.shape, BF16)],
        [
            pltpu.VMEM((parts, own * heads * steps, HEAD_DIM), BF16),
            pltpu.VMEM((parts, heads, tall, HEAD_DIM), F32),
            pltpu.VMEM((own, GROUP * steps, cache.shape[3]), F32),
            pltpu.VMEM((own, 2 * GROUP * steps, cache.shape[3]), BF16),
            pltpu.VMEM((own, GROUP * steps, cache.shape[3]), F32),
            pltpu.SemaphoreType.DMA((early,)),
        ],
        alias={parts + 2: parts + 1},
    )
    attended, buffers = attended[:parts], [(0, attended[parts])]
    buffers += [
        (
            early,
            call(
                functools.partial(fetch_kernel, first=early),
                "fetch",
                [(ANY, attended[0]), (HBM, weight)],
                [pltpu.VMEM((fetched, depth, wide), BF16)],
                [pltpu.SemaphoreType.DMA((fetched,))],
                cost=pl.CostEstimate(
                    flops=0, bytes_accessed=2 * fetched * depth * wide, transcendentals=0
                ),
            )[0],
        )
    ]
    attended, factors = lax.optimization_barrier((list(attended), factors))
    factors |= {k ^ 1: swap(v, "fsdp", 1) for k, v in list(factors.items())}
    got = {k: swap(attended[k], "tensor", k) for k in range(parts - 1, 0, -1)}
    attended = [attended[0]] + [got[k] for k in range(1, parts)]

    order = sorted(range(parts), key=lambda k: format(k, "08b")[::-1])
    attended = [attended[k] for k in order]

    def reduce(keep, send):
        bit = 1
        while True:
            got = swap(send, "tensor", bit)
            bit *= 2
            if bit == sets:
                return keep, got
            both = keep + got.astype(F32)
            half = both.shape[0] // 2
            keep, send = both[:half], both[half:].astype(BF16)

    def reduce_low(keep, send):
        bit = 1
        while True:
            both = fold_low(keep, swap(send, "tensor", bit))
            bit *= 2
            if bit == sets:
                return both
            half = both.shape[0] // 2
            keep, send = both[:half], jnp.concatenate(split(both[half:]), axis=1)

    keep, send, buffers = project(attended, weight, buffers, 0, spread, half)
    ordered = cut % HEAD_DIM != 0
    if sets == 2 and not ordered:
        inner = (spread * RANK * cut) // (2 * tall)
        low_keep, ups, handoff = call(
            functools.partial(handoff_kernel, parts=parts, slot=slot),
            "handoff",
            [(VMEM, a) for a in (send, *attended, *[factors[k] for k in range(spread)])],
            [
                shape_of((2 * tall, RANK), F32),
                shape_of((spread, RANK, cut), BF16),
                shape_of((2 * tall, half_width + inner + 2 * RANK), BF16),
            ],
            [pltpu.VMEM((RANK, depth), BF16)],
        )
        handoff = swap(handoff, "tensor", 1)
        far, message, low = call(
            join_kernel,
            "join",
            [(VMEM, a) for a in (keep, low_keep, handoff)],
            [
                shape_of((tall, half_width), F32),
                shape_of((tall, half_width + 4 * RANK), BF16),
                shape_of((2 * tall, RANK), F32),
            ],
        )
        up_sets = {0: ups, 1: handoff}
    else:
        far_keep, far_got = reduce(keep, send)

        down_rows, ups = call(
            functools.partial(collect_kernel, slot=slot),
            "collect",
            [(ANY, keep)] + [(VMEM, factors[k]) for k in range(spread)],
            [shape_of((RANK, depth), BF16), shape_of((spread, RANK, cut), BF16)],
        )
        low_keep, low_send = call(
            lower_kernel,
            "lower",
            [(VMEM, a) for a in (*attended, down_rows)],
            [shape_of((sets * tall, RANK), F32), shape_of((sets * tall, 2 * RANK), BF16)],
        )
        low = reduce_low(low_keep, low_send)
        if ordered:
            ups = lax.all_gather(up, ("fsdp", "tensor"), axis=1, tiled=True)
            ups = ups.reshape(RANK, spread, 2, wide)
            top = lax.axis_index("tensor") // sets
            ups = lax.dynamic_index_in_dim(ups, top, 2, keepdims=False)
            up_sets = {0: ups.reshape(RANK, half_width)}
        else:
            up_sets = {0: ups}
            bit = sets // 2
            while bit:
                up_sets |= {k ^ bit: swap(u, "tensor", bit) for k, u in list(up_sets.items())}
                bit //= 2
        far = far_keep + far_got.astype(F32)
        low_parts = jnp.concatenate(split(low), axis=1)
        message = jnp.concatenate([far[tall:].astype(BF16), low_parts[tall:], low_parts[:tall]], axis=1)
        far = far[:tall]

    near = []

    def add_near(low, high, ahead):
        nonlocal buffers
        keep, send, buffers = project(attended, weight, buffers, low, high, ahead)
        near.append(reduce(keep, send))

    a, b = spread + quarter, 2 * spread - quarter
    add_near(spread, a, quarter)
    message, attended = lax.optimization_barrier((message, attended))
    message = swap(message, "tensor", sets)
    add_near(a, b, quarter)
    add_near(b, 2 * spread, 0)
    near_got, low_got = message[:, :half_width], message[:, half_width:]

    ups = [up_sets[k] for k in range(len(up_sets))]
    near_keep, near_send = call(
        functools.partial(adapt_kernel, pieces=len(near), sets=sets, ordered=ordered),
        "adapt",
        [(VMEM, a) for a in (low, low_got, *[k for k, _ in near], *[g for _, g in near], *ups)],
        [shape_of((tall, half_width), F32), shape_of((tall, half_width), BF16)],
        [pltpu.VMEM((2 * tall, half_width), F32)],
    )
    far_got = swap(near_send, "tensor", sets)

    return call(
        functools.partial(finish_kernel, own=own, steps=steps, strips=spread),
        "finish",
        [(VMEM, a) for a in (far, far_got, near_keep, near_got)],
        [shape_of((steps, own, weight.shape[1]), BF16)],
    )[0]


def solution(mesh):
    return jax.shard_map(
        shards,
        mesh=mesh,
        in_specs=(
            P(None, ("groups", "fsdp"), "tensor"),
            P(("groups", "fsdp", "tensor"), None, None, None, None),
            P(None, ("groups", "fsdp"), "tensor"),
            P(("groups", "fsdp", "tensor")),
            P("tensor", None),
            P("tensor", "fsdp"),
            P(None, ("fsdp", "tensor")),
        ),
        out_specs=P(None, ("groups", "fsdp", "tensor"), None),
        check_vma=False,
    )
```
